256 devices in a mesh: grp: 4 (over z_hi), seq: 16 (over x, z_lo, core), rep: 4 (over y).
Axes of the slice: x: 4, y: 4, z: 8 (z_hi: 4, z_lo: 2; z = z_hi * 2 + z_lo), core: 2. Of those that a mesh axis runs over, the one named last changes fastest.
Arguments:
- hidden: bfloat16 [4, 4, 2048, 3072], P('rep', 'grp', 'seq'), may hold values from -6 to 6
- queries_keys: bfloat16 [4, 4, 2048, 2, 2048], P('rep', 'grp', 'seq'), may hold values from -10 to 10
- values: bfloat16 [4, 4, 2048, 2048], P('rep', 'grp', 'seq'), may hold values from -6 to 6
- text_len: int32 [4, 4], P('rep', 'grp'), may hold values from 64 to 256
- timestep: int32 [4, 4], P('rep', 'grp'), may hold values from 0 to 63
- gate_table: float32 [64, 3072], replicated, may hold values from 0.5 to 1.5
- w_out: bfloat16 [2, 2048, 3072], P(None, 'seq', 'rep'), may hold values from -0.125 to 0.125
- w_zero: bfloat16 [3072, 3072], P('seq', 'grp'), may hold values from -0.109375 to 0.109375
- cotangent: bfloat16 [4, 4, 2048, 3072], P('rep', 'grp', 'seq'), may hold values from -6 to 6
Outputs:
- final: bfloat16 [4, 4, 2048, 3072], P('rep', 'grp', 'seq')
- ctrl_grad: bfloat16 [4, 2048, 3072], P('rep', 'seq', 'grp')
- grad_zero: float32 [3072, 3072], P(('seq', 'rep'), 'grp')
The draws below stay inside these ranges and needn't reach their ends.
All inputs are finite; a program needn't handle non-finite values.
Results may differ from the reference program's by a relative error of at most 0.019.
Values may be sent and summed in bfloat16 or wider, within the bound.
No kernel may reach another device: no remote copies, remote signals or barrier semaphores. Data moves between devices by JAX's collectives and lax.ppermute only.
A program may use at most 128 MiB of HBM per device.

```python
import math
import jax
import jax.numpy as jnp
from jax import lax

D = 3072
H = 16
HEAD = 128
STEPS = 64
L = 2048
TXT = 256
HD = 2048
N_GRP = 4
N_REP = 4


def plant_pairs(base, sign_key, place_key, strengths):
    streams = base.shape[0]
    sign_table = jnp.where(jax.random.bernoulli(sign_key, 0.5, (streams, 3, HD)), 1.0, -1.0)

    def pick_places(sub_key):
        return jax.random.permutation(sub_key, L - TXT)[:9]
    placed = jax.vmap(pick_places)(jax.random.split(place_key, streams)) + TXT
    position = jnp.arange(L)
    leading_mask = (jnp.arange(HD) % HEAD == 0).astype(jnp.float32)
    queries = base[:, :, 0]
    key_rows = base[:, :, 1]
    for group_index in range(3):
        strength = strengths[group_index]
        shortfall = 2.0 * math.sqrt(HEAD) / strength
        direction = sign_table[:, group_index][:, None, :]
        query_here = (position[None, :] == placed[:, group_index][:, None])[:, :, None]
        first_here = (position[None, :] == placed[:, 3 + group_index][:, None])[:, :, None]
        second_here = (position[None, :] == placed[:, 6 + group_index][:, None])[:, :, None]
        queries = jnp.where(query_here, strength * direction, queries)
        key_rows = jnp.where(first_here, 10.0 * direction, key_rows)
        key_rows = jnp.where(second_here, (10.0 - shortfall * leading_mask)[None, None, :] * direction, key_rows)
    return jnp.stack([queries, key_rows], axis=2)


def draw_queries_keys(key, part):
    key = jax.random.fold_in(key, 7)
    base_key, sign_key, place_key = jax.random.split(key, 3)
    streams = N_REP * N_GRP
    base = jnp.clip(2.0 * jax.random.normal(base_key, (streams, L, 2, HD), jnp.float32), -8.0, 8.0)
    strengths = (10.0, 8.0, 6.0)
    planted = plant_pairs(base, sign_key, place_key, strengths)
    return planted.reshape(N_REP, N_GRP, L, 2, HD).astype(jnp.bfloat16)


def with_ends(entries, rng, smallest, largest):
    extent = entries.shape
    place = [jax.random.randint(jax.random.fold_in(rng, axis), (), 0, extent[axis]) for axis in range(len(extent))]
    entries = entries.at[tuple(place)].set(smallest)
    longest = extent.index(max(extent))
    place[longest] = (place[longest] + 1) % extent[longest]
    return entries.at[tuple(place)].set(largest)


def steps_of(own_key, extent, cuts, smallest, largest):
    loudness, own = 1.0, jax.random.fold_in(own_key, 6)
    for axis_at, shards_of in cuts:
        heights = jnp.exp(jax.random.uniform(jax.random.fold_in(own, axis_at), (shards_of,), jnp.float32, smallest / len(cuts), largest / len(cuts)))
        loudness = loudness * jnp.repeat(heights, extent[axis_at] // shards_of).reshape([-1 if axis == axis_at else 1 for axis in range(len(extent))])
    return loudness


def centred(own_key, shape, scale, bound, pieces=(), kind=jnp.bfloat16):
    factor_of = steps_of(own_key, shape, pieces, -0.22, 0.18) if pieces else 1.0
    values = jax.random.normal(own_key, shape, jnp.float32) * scale * factor_of
    return jnp.minimum(jnp.maximum(values, -bound), bound).astype(kind)


def setup_inputs(seed: int = 0) -> dict:
    key_of = jax.random.split(jax.random.key(seed), 10)
    hidden = centred(key_of[0], (N_REP, N_GRP, L, D), 1.0, 6.0, ((0, 4), (1, 4), (2, 16)))
    queries_keys = draw_queries_keys(jax.random.fold_in(key_of[9], 71), 0)
    values = centred(key_of[2], (N_REP, N_GRP, L, HD), 1.0, 6.0, ((0, 4), (1, 4), (2, 16)))
    text_len = with_ends(jax.random.randint(key_of[3], (N_REP, N_GRP), TXT // 4, TXT + 1), jax.random.fold_in(key_of[3], 1), TXT // 4, TXT).astype(jnp.int32)
    timestep = with_ends(jax.random.randint(key_of[4], (N_REP, N_GRP), 0, STEPS), jax.random.fold_in(key_of[4], 1), 0, STEPS - 1).astype(jnp.int32)
    gate_table = jnp.clip(jax.random.uniform(key_of[5], (STEPS, D), jnp.float32, 0.5, 1.5), 0.5, 1.5)
    w_out = centred(key_of[6], (2, HD, D), HD ** -0.5, 0.125, ((1, 16), (2, 4)))
    w_zero = centred(key_of[7], (D, D), D ** -0.5, 0.109375, ((0, 16), (1, 4)))
    cotangent = centred(key_of[8], (N_REP, N_GRP, L, D), 1.0, 6.0, ((0, 4), (1, 4), (2, 16)))
    return dict(hidden=hidden, queries_keys=queries_keys, values=values, text_len=text_len, timestep=timestep, gate_table=gate_table, w_out=w_out, w_zero=w_zero, cotangent=cotangent)


def attend(qk, vals, tlen):
    length = qk.shape[0]
    queries = qk[:, 0].reshape(length, H, HEAD)
    keys = qk[:, 1].reshape(length, H, HEAD).astype(jnp.float32)
    vv = vals.reshape(length, H, HEAD).astype(jnp.float32)
    position = jnp.arange(length)
    valid = (position >= TXT) | (position < tlen)
    block = math.gcd(length, 512)
    blocks = queries.reshape(length // block, block, H, HEAD)

    def one_block(q_block):
        scores = jnp.einsum('bhe,khe->hbk', q_block.astype(jnp.float32), keys) * (HEAD ** -0.5)
        scores = jnp.where(valid[None, None, :], scores, -jnp.inf)
        weights = jax.nn.softmax(scores, axis=-1).astype(jnp.bfloat16)
        result = jnp.einsum('hbk,khe->bhe', weights.astype(jnp.float32), vv)
        return result.astype(jnp.bfloat16).reshape(block, H * HEAD)

    return lax.map(one_block, blocks).reshape(length, H * HEAD)


def reference(hidden, queries_keys, values, text_len, timestep, gate_table, w_out, w_zero, cotangent):
    slots = N_REP * N_GRP
    roles = (jnp.arange(slots) % N_GRP > 0).astype(jnp.int32)

    def slot_out(items):
        h_rows, qk, vals, tlen, tstep, role = items
        attn = attend(qk, vals, tlen)
        weight = jnp.where(role > 0, w_out[1], w_out[0])
        proj = jnp.dot(attn, weight, preferred_element_type=jnp.float32)
        return (h_rows.astype(jnp.float32) + gate_table[tstep] * proj).astype(jnp.bfloat16)

    outs = lax.map(slot_out, (hidden.reshape(slots, L, D), queries_keys.reshape(slots, L, 2, HD),
                              values.reshape(slots, L, HD), text_len.reshape(slots),
                              timestep.reshape(slots), roles))
    outs = outs.reshape(N_REP, N_GRP, L, D)
    control = outs[:, 0].reshape(N_REP * L, D)
    resid = jnp.dot(control, w_zero, preferred_element_type=jnp.float32).astype(jnp.bfloat16)
    resid = resid.reshape(N_REP, 1, L, D)
    mains = (outs[:, 1:].astype(jnp.float32) + resid.astype(jnp.float32)).astype(jnp.bfloat16)
    final = jnp.concatenate([outs[:, :1], mains], axis=1)
    csum = jnp.sum(cotangent[:, 1:].astype(jnp.float32), axis=1).astype(jnp.bfloat16).reshape(N_REP * L, D)
    own_cot = cotangent[:, 0].reshape(N_REP * L, D).astype(jnp.float32)
    width = D // N_GRP
    total = jnp.zeros((N_REP * L, D), jnp.float32)
    for block_index in range(N_GRP):
        lo = block_index * width
        term = jnp.dot(csum[:, lo:lo + width], w_zero[:, lo:lo + width].T, preferred_element_type=jnp.float32)
        if block_index == 0:
            term = term + own_cot
        total = total + term.astype(jnp.bfloat16).astype(jnp.float32)
    ctrl_grad = total.astype(jnp.bfloat16).reshape(N_REP, L, D)
    grad_zero = jnp.dot(control.T, csum, preferred_element_type=jnp.float32)
    return final, ctrl_grad, grad_zero
```

```python
import functools
import math

import jax
import jax.numpy as jnp
from jax import lax
from jax.experimental import pallas as pl
from jax.experimental.pallas import tpu as pltpu
from jax.sharding import Mesh, PartitionSpec as P

H = 16
HEAD = 128
SIZES = {"grp": 4, "x": 4, "zl": 2, "core": 2, "rep": 4}
SEQ = ("x", "zl", "core")
BF = jnp.bfloat16
F32 = jnp.float32
MIB = 1 << 20


def send(value, axis, pairs):
    return lax.ppermute(value, axis, pairs)


def shift(value, axis, step):
    n = SIZES[axis]
    return lax.ppermute(value, axis, [(i, (i + step) % n) for i in range(n)])


def attend_kernel(tlen_ref, q_ref, k_ref, v_ref, o_ref, wide_ref, *, text_slots, scale):
    @pl.when(pl.program_id(0) == 0)
    def _():
        length = wide_ref.shape[0]
        wide_ref[:, :HEAD] = v_ref[...].reshape(length, HEAD)
        wide_ref[:, HEAD:] = jnp.ones((length, HEAD), BF)

    rows = o_ref.shape[0]
    q = q_ref[...].reshape(rows, HEAD)
    length = wide_ref.shape[0]
    k = k_ref[...].reshape(length, HEAD)
    s = lax.dot_general(q, k, (((1,), (1,)), ((), ())), preferred_element_type=F32)
    place = lax.broadcasted_iota(jnp.int32, (rows, text_slots), 1)
    head = jnp.where(place < tlen_ref[0, 0], s[:, :text_slots], -jnp.inf)
    tail = s[:, text_slots:]
    top = jnp.maximum(
        jnp.max(head, axis=1, keepdims=True), jnp.max(tail, axis=1, keepdims=True)
    )
    factor = scale * math.log2(math.e)
    p_head = jnp.exp2((head - top) * factor).astype(BF)
    p_tail = jnp.exp2((tail - top) * factor).astype(BF)
    both = jnp.dot(p_head, wide_ref[:text_slots, :], preferred_element_type=F32) + jnp.dot(
        p_tail, wide_ref[text_slots:, :], preferred_element_type=F32
    )
    o_ref[...] = (both[:, :HEAD] / both[:, HEAD:]).astype(BF)


def attend(qkv, tlen):
    blocks, _, per, _ = qkv.shape
    length = blocks * per
    q_blocks = 2
    rows = q_blocks * per
    whole = lambda part: pl.BlockSpec((blocks, None, per, HEAD), lambda i: (0, part, 0, 0))
    return pl.pallas_call(
        functools.partial(attend_kernel, text_slots=length // 8, scale=HEAD ** -0.5),
        grid=(length // rows,),
        in_specs=[
            pl.BlockSpec(memory_space=pltpu.SMEM),
            pl.BlockSpec((q_blocks, None, per, HEAD), lambda i: (i, 0, 0, 0)),
            whole(1),
            whole(2),
        ],
        out_specs=pl.BlockSpec((rows, HEAD), lambda i: (i, 0)),
        out_shape=jax.ShapeDtypeStruct((length, HEAD), BF),
        scratch_shapes=[pltpu.VMEM((length, 2 * HEAD), BF)],
        compiler_params=pltpu.CompilerParams(vmem_limit_bytes=40 * MIB),
        cost_estimate=pl.CostEstimate(
            flops=6 * length * length * HEAD,
            bytes_accessed=8 * length * HEAD,
            transcendentals=length * length,
        ),
        name="attend",
    )(tlen, qkv, qkv, qkv)


def project_kernel(place_ref, a_ref, y0, y1, y3, y2a, y2b, x0, x1, x3, x2a, x2b, own_ref, other_ref, wide_ref):
    half = own_ref.shape[0]
    x, zl, core, rep = place_ref[0], place_ref[1], place_ref[2], place_ref[3]
    mine = pl.multiple_of(core * half, half)
    theirs = pl.multiple_of((1 - core) * half, half)
    for at, step in enumerate((0, 1, 3, 2)):
        for other_zl in range(2):
            head = lax.rem(x + 4 - step, 4) * 2 + (1 - zl if other_zl else zl)
            lanes = slice((2 * at + other_zl) * HEAD, (2 * at + other_zl + 1) * HEAD)
            wide_ref[:half, lanes] = a_ref[head, pl.ds(mine, half), :]
            wide_ref[half:, lanes] = a_ref[head, pl.ds(theirs, half), :]
    wide_y, wide_x, depth = y0.shape[1], x0.shape[2], x0.shape[1]
    block = wide_y + wide_x

    def times(lanes, w):
        return jnp.dot(wide_ref[:, lanes], w, preferred_element_type=F32)

    for at, step in enumerate((0, 1, 3, 2)):
        start = lax.rem(rep + 4 - step, 4) * block
        if step == 2:
            deep = y2a.shape[0]
            total = times(slice(0, deep), y2a[...]) + times(slice(deep, 2 * deep), y2b[...])
        else:
            total = times(slice(None), (y0, y1, None, y3)[step][...])
        place = pl.ds(pl.multiple_of(start, HEAD), wide_y)
        own_ref[:, place] = total[:half]
        other_ref[:, place] = total[half:].astype(BF)
        total = 0.0
        for k, piece in enumerate((x0, x1, x3)):
            total = total + times(slice(k * depth, (k + 1) * depth), piece[at])
        far = x2a[at] if at < 2 else x2b[at - 2]
        total = total + times(slice(3 * depth, 4 * depth), far)
        place = pl.ds(pl.multiple_of(start + wide_y, HEAD), wide_x)
        own_ref[:, place] = total[:half]
        other_ref[:, place] = total[half:].astype(BF)


def project(place, attn, by_y, by_x):
    heads, rows, _ = attn.shape
    half = rows // 2
    columns = 4 * (by_y[0].shape[1] + by_x[0].shape[2])
    vmem = pl.BlockSpec(memory_space=pltpu.VMEM)
    return pl.pallas_call(
        project_kernel,
        in_specs=[pl.BlockSpec(memory_space=pltpu.SMEM)] + [vmem] * 11,
        out_specs=[vmem, vmem],
        out_shape=[
            jax.ShapeDtypeStruct((half, columns), F32),
            jax.ShapeDtypeStruct((half, columns), BF),
        ],
        scratch_shapes=[pltpu.VMEM((rows, heads * HEAD), BF)],
        compiler_params=pltpu.CompilerParams(vmem_limit_bytes=40 * MIB),
        cost_estimate=pl.CostEstimate(
            flops=2 * rows * heads * HEAD * columns,
            bytes_accessed=2 * heads * HEAD * columns,
            transcendentals=0,
        ),
        name="project",
    )(place, attn, *by_y, *by_x)


def ring_gather(value, axis, split):
    below, above = shift(value, axis, 1), shift(value, axis, -1)
    far_a = shift(below[:split], axis, 1)
    far_b = shift(above[split:], axis, -1)
    return value, below, above, far_a, far_b


def gate(*values):
    return lax.optimization_barrier(values)


def grad_kernel(c0, c1, c2, c3, s0, s1, s2, s3, o_ref, ctl_ref, sum_ref):
    rows = c0.shape[0]
    for at, (c, s) in enumerate(((c0, s0), (c1, s1), (c2, s2), (c3, s3))):
        ctl_ref[at * rows : (at + 1) * rows, :] = c[...]
        sum_ref[at * rows : (at + 1) * rows, :] = s[...]
    o_ref[...] = lax.dot_general(
        ctl_ref[...], sum_ref[...], (((0,), (0,)), ((), ())), preferred_element_type=F32
    ).astype(BF)


def grad_partial(ctl, csum):
    rows, width = ctl[0].shape
    vmem = pl.BlockSpec(memory_space=pltpu.VMEM)
    return pl.pallas_call(
        grad_kernel,
        in_specs=[vmem] * 8,
        out_specs=vmem,
        out_shape=jax.ShapeDtypeStruct((width, width), BF),
        scratch_shapes=[pltpu.VMEM((4 * rows, width), BF)] * 2,
        compiler_params=pltpu.CompilerParams(vmem_limit_bytes=40 * MIB),
        cost_estimate=pl.CostEstimate(
            flops=8 * rows * width * width, bytes_accessed=18 * rows * width, transcendentals=0
        ),
        name="grad_partial",
    )(*ctl, *csum)


def pick(blocks, index):
    return lax.dynamic_index_in_dim(blocks, index, 0, keepdims=False)


def shards(hidden, queries_keys, values, text_len, timestep, gate_table, w_out, w_zero, cotangent):
    g = lax.axis_index("grp")
    x = lax.axis_index("x")
    core = lax.axis_index("core")
    rep = lax.axis_index("rep")
    zl = lax.axis_index("zl")
    is_control = g == 0
    n_grp, n_x, n_rep = SIZES["grp"], SIZES["x"], SIZES["rep"]
    tok, width = hidden.shape[2], w_zero.shape[1]

    w_sel = jnp.where(is_control, w_out[0], w_out[1])
    pair = queries_keys[0, 0].reshape(tok, 2, H, HEAD).transpose(2, 1, 0, 3)
    vals = values[0, 0].reshape(tok, 1, H, HEAD).transpose(2, 1, 0, 3)
    qkv, w_pair = gate(
        jnp.concatenate([pair, vals], axis=1), jnp.concatenate([w_sel, shift(w_sel, "zl", 1)])
    )

    wide = 512
    first, second = w_pair[:, :wide], w_pair[:, wide:]
    qkv = lax.all_to_all(qkv, SEQ, split_axis=0, concat_axis=0, tiled=True)
    over_x = [first] + [shift(first, "x", step) for step in (1, 3, 2)]
    over_y = [second] + [shift(second, "rep", step) for step in (1, 3, 2)]
    qkv, over_x, over_y, cot, zero_own = gate(qkv, over_x, over_y, cotangent[0, 0], w_zero)

    zero_block = lax.all_gather(zero_own, SEQ, axis=0, tiled=True)
    over_x, over_y = jnp.concatenate(over_x), jnp.stack(over_y)
    by_y = ring_gather(over_x, "rep", over_x.shape[0] // 2)
    by_x = ring_gather(over_y, "x", over_y.shape[0] // 2)

    def cot_block(index):
        return lax.dynamic_slice_in_dim(cot, index * width, width, axis=1)

    csum = jnp.where(is_control, 0.0, cot_block(g).astype(F32))
    for step in range(1, n_grp):
        pairs = [(i, (i + step) % n_grp) for i in range(1, n_grp)]
        got = send(cot_block((g + step) % n_grp), "grp", pairs)
        csum = csum + got.astype(F32)
    attn, csum = gate(attend(qkv, text_len), csum.astype(BF))

    heads = lax.all_to_all(
        attn.reshape(8, 2 * tok, HEAD), ("x", "zl"), split_axis=0, concat_axis=0, tiled=True
    )
    own, other = project(jnp.stack([x, zl, core, rep]), heads, by_y, by_x)
    other = shift(other, "core", 1)
    level = lax.dynamic_slice_in_dim(gate_table, timestep[0, 0], 1, axis=0)
    out = (hidden[0, 0].astype(F32) + level * (own + other.astype(F32))).astype(BF)

    out, csum = gate(out, csum)
    top, low = out[: tok // 2], out[tok // 2 :]
    csum_x = [csum] + [shift(csum, "x", step) for step in range(1, n_x)]
    right = send(top, "grp", [(0, 1)])
    left = send(low, "grp", [(0, 3)])
    right, left, top, low = gate(right, left, top, low)
    low_far = send(jnp.where(is_control, low, left), "grp", [(0, 1), (3, 2)])
    top_far = send(jnp.where(is_control, top, right), "grp", [(0, 3), (1, 2)])
    low_far, top_far, csum_x, zero_block = gate(low_far, top_far, csum_x, zero_block)
    control = jnp.concatenate(
        [
            jnp.where(is_control, top, jnp.where(g == 1, right, top_far)),
            jnp.where(is_control, low, jnp.where(g == 3, left, low_far)),
        ]
    )

    resid = jnp.dot(control, zero_block, preferred_element_type=F32).astype(BF)
    resid, control = gate(resid, control)
    parts = [resid] + [
        send(resid, "grp", [(i, (i + step) % n_grp) for i in range(n_grp) if (i + step) % n_grp])
        for step in range(1, n_grp)
    ]
    columns = []
    for j in range(n_grp):
        block = parts[0]
        for step in range(1, n_grp):
            block = jnp.where((g - step) % n_grp == j, parts[step], block)
        columns.append(block)
    resid_all = jnp.concatenate(columns, axis=1)
    final = jnp.where(is_control, out, (out.astype(F32) + resid_all.astype(F32)).astype(BF))

    def ctl_block(index):
        return lax.dynamic_slice_in_dim(control, index * width, width, axis=1)

    ctl_x = [ctl_block(x)] + [
        shift(ctl_block((x + step) % n_x), "x", step) for step in range(1, n_x)
    ]
    partial = grad_partial(ctl_x, csum_x)
    partial, csum = gate(partial, csum)
    term = lax.dot_general(csum, zero_block, (((1,), (1,)), ((), ())), preferred_element_type=F32)
    term = jnp.where(is_control, term + cotangent[0, 0].astype(F32), term).astype(BF)

    def term_block(index):
        return lax.dynamic_slice_in_dim(term, index * width, width, axis=1)

    ctrl = term_block(g).astype(F32)
    for step in range(1, n_grp):
        ctrl = ctrl + shift(term_block((g + step) % n_grp), "grp", step).astype(F32)
    ctrl_grad = ctrl.astype(BF)

    rows = width // 16
    partial = partial.reshape(2, 2, n_rep * rows, width).transpose(1, 0, 2, 3)
    mine = pick(partial, core).astype(F32)
    got = shift(pick(partial, 1 - core), "core", 1)
    over_rep = (mine + got.astype(F32)).reshape(2, n_rep, rows, width).transpose(1, 0, 2, 3)
    grad = pick(over_rep, rep)
    for step in range(1, n_rep):
        got = shift(pick(over_rep, (rep + step) % n_rep).astype(BF), "rep", step)
        grad = grad + got.astype(F32)
    mine = pick(grad, zl)
    got = shift(pick(grad, 1 - zl).astype(BF), "zl", 1)
    grad_zero = mine + got.astype(F32)
    return (final[None, None], ctrl_grad[None], grad_zero)


def solution(mesh):
    split = Mesh(mesh.devices.reshape(4, 4, 2, 2, 4), ("grp", "x", "zl", "core", "rep"))
    placed = (
        P("rep", "grp", SEQ, None),
        P("rep", "grp", SEQ, None, None),
        P("rep", "grp", SEQ, None),
        P("rep", "grp"),
        P("rep", "grp"),
        P(),
        P(None, SEQ, "rep"),
        P(SEQ, "grp"),
        P("rep", "grp", SEQ, None),
    )
    return jax.shard_map(
        shards,
        mesh=split,
        in_specs=placed,
        out_specs=(P("rep", "grp", SEQ, None), P("rep", SEQ, "grp"), P((*SEQ, "rep"), "grp")),
        check_vma=False,
    )
```

```python
import functools
import math

import jax
import jax.numpy as jnp
from jax import lax
from jax.experimental import pallas as pl
from jax.experimental.pallas import tpu as pltpu
from jax.sharding import Mesh, PartitionSpec as P

H = 16
HEAD = 128
SIZES = {"grp": 4, "x": 4, "zl": 2, "core": 2, "rep": 4}
SEQ = ("x", "zl", "core")
BF = jnp.bfloat16
F32 = jnp.float32
MIB = 1 << 20


def send(value, axis, pairs):
    return lax.ppermute(value, axis, pairs)


def shift(value, axis, step):
    n = SIZES[axis]
    return lax.ppermute(value, axis, [(i, (i + step) % n) for i in range(n)])


def attend_kernel(tlen_ref, q_ref, k_ref, v_ref, o_ref, wide_ref, *, text_slots, scale):
    @pl.when(pl.program_id(0) == 0)
    def _():
        length = wide_ref.shape[0]
        wide_ref[:, :HEAD] = v_ref[...].reshape(length, HEAD)
        wide_ref[:, HEAD:] = jnp.ones((length, HEAD), BF)

    rows = o_ref.shape[0]
    q = q_ref[...].reshape(rows, HEAD)
    length = wide_ref.shape[0]
    k = k_ref[...].reshape(length, HEAD)
    s = lax.dot_general(q, k, (((1,), (1,)), ((), ())), preferred_element_type=F32)
    place = lax.broadcasted_iota(jnp.int32, (rows, text_slots), 1)
    head = jnp.where(place < tlen_ref[0, 0], s[:, :text_slots], -jnp.inf)
    tail = s[:, text_slots:]
    top = jnp.maximum(
        jnp.max(head, axis=1, keepdims=True), jnp.max(tail, axis=1, keepdims=True)
    )
    factor = scale * math.log2(math.e)
    p_head = jnp.exp2((head - top) * factor).astype(BF)
    p_tail = jnp.exp2((tail - top) * factor).astype(BF)
    both = jnp.dot(p_head, wide_ref[:text_slots, :], preferred_element_type=F32) + jnp.dot(
        p_tail, wide_ref[text_slots:, :], preferred_element_type=F32
    )
    o_ref[...] = (both[:, :HEAD] / both[:, HEAD:]).astype(BF)


def attend(qkv, tlen):
    blocks, _, per, _ = qkv.shape
    length = blocks * per
    q_blocks = 2
    rows = q_blocks * per
    whole = lambda part: pl.BlockSpec((blocks, None, per, HEAD), lambda i: (0, part, 0, 0))
    return pl.pallas_call(
        functools.partial(attend_kernel, text_slots=length // 8, scale=HEAD ** -0.5),
        grid=(length // rows,),
        in_specs=[
            pl.BlockSpec(memory_space=pltpu.SMEM),
            pl.BlockSpec((q_blocks, None, per, HEAD), lambda i: (i, 0, 0, 0)),
            whole(1),
            whole(2),
        ],
        out_specs=pl.BlockSpec((rows, HEAD), lambda i: (i, 0)),
        out_shape=jax.ShapeDtypeStruct((length, HEAD), BF),
        scratch_shapes=[pltpu.VMEM((length, 2 * HEAD), BF)],
        compiler_params=pltpu.CompilerParams(vmem_limit_bytes=40 * MIB),
        cost_estimate=pl.CostEstimate(
            flops=6 * length * length * HEAD,
            bytes_accessed=8 * length * HEAD,
            transcendentals=length * length,
        ),
        name="attend",
    )(tlen, qkv, qkv, qkv)


def project_kernel(zl_ref, a_ref, w_ref, own_ref, other_ref, a_held, wide_ref, held, sems, *, first):
    heads, half = held.shape[0], own_ref.shape[0]
    count, _, width = held.shape[1:]
    load = pltpu.make_async_copy(a_ref, a_held, sems.at[heads])
    load.start()
    copies = [
        pltpu.make_async_copy(w_ref.at[h, pl.ds(first, count)], held.at[h], sems.at[h])
        for h in range(heads)
    ]
    for copy in copies:
        copy.start()
    mine = pl.multiple_of(zl_ref[0] * half, half)
    theirs = pl.multiple_of((1 - zl_ref[0]) * half, half)
    load.wait()
    for h in range(heads):
        lanes = slice(h * HEAD, (h + 1) * HEAD)
        wide_ref[:half, lanes] = a_held[h, pl.ds(mine, half), :]
        wide_ref[half:, lanes] = a_held[h, pl.ds(theirs, half), :]
    for copy in copies:
        copy.wait()
    for j in range(count):
        w = held[:, j].reshape(heads * HEAD, width)
        total = jnp.dot(wide_ref[...], w, preferred_element_type=F32)
        lanes = slice(j * width, (j + 1) * width)
        own_ref[:, lanes] = total[:half]
        other_ref[:, lanes] = total[half:].astype(BF)


def project(zl, attn, weight, first, count):
    heads, rows, _ = attn.shape
    _, _, depth, width = weight.shape
    half = rows // 2
    vmem, anywhere = pl.BlockSpec(memory_space=pltpu.VMEM), pl.BlockSpec(memory_space=pl.ANY)
    return pl.pallas_call(
        functools.partial(project_kernel, first=first),
        in_specs=[pl.BlockSpec(memory_space=pltpu.SMEM), anywhere, anywhere],
        out_specs=[vmem, vmem],
        out_shape=[
            jax.ShapeDtypeStruct((half, count * width), F32),
            jax.ShapeDtypeStruct((half, count * width), BF),
        ],
        scratch_shapes=[
            pltpu.VMEM(attn.shape, BF),
            pltpu.VMEM((rows, heads * HEAD), BF),
            pltpu.VMEM((heads, count, depth, width), BF),
            pltpu.SemaphoreType.DMA((heads + 1,)),
        ],
        compiler_params=pltpu.CompilerParams(vmem_limit_bytes=60 * MIB),
        cost_estimate=pl.CostEstimate(
            flops=2 * rows * heads * HEAD * count * width,
            bytes_accessed=2 * heads * HEAD * count * width,
            transcendentals=0,
        ),
        name="project",
    )(zl, attn, weight)


def ring_gather(value, axis):
    return [value] + [shift(value, axis, step) for step in range(1, 4)]


def gate(*values):
    return lax.optimization_barrier(values)


def fetch_zero(zero_ref, held, sems):
    copies = []
    for x in range(4):
        for core in range(2):
            for rep in range(4):
                target = held.at[x, :, core, rep]
                copies.append(pltpu.make_async_copy(zero_ref.at[x, core, rep], target, sems.at[x, core, rep]))
    for copy in copies:
        copy.start()
    return copies


def block_of(held, copies, j):
    for copy in copies[8 * j : 8 * (j + 1)]:
        copy.wait()
    width = held.shape[-1]
    return held[j].reshape(width, width)


def resid_kernel(ctl_ref, zero_ref, o_ref, held, sems):
    copies = fetch_zero(zero_ref, held, sems)
    for j in range(4):
        w = block_of(held, copies, j)
        o_ref[j] = jnp.dot(ctl_ref[...], w, preferred_element_type=F32).astype(BF)


def term_kernel(csum_ref, cot_ref, zero_ref, o_ref, held, sems):
    copies = fetch_zero(zero_ref, held, sems)
    total = 0.0
    for j in range(4):
        term = lax.dot_general(
            csum_ref[j],
            block_of(held, copies, j),
            (((1,), (1,)), ((), ())),
            preferred_element_type=F32,
        )
        if j == 0:
            term = term + cot_ref[...].astype(F32)
        total = total + term.astype(BF).astype(F32)
    o_ref[...] = total.astype(BF)


def with_zero(kernel, dense, zero, shape, name):
    _, _, reps, _, slab, width = zero.shape
    vmem = pl.BlockSpec(memory_space=pltpu.VMEM)
    return pl.pallas_call(
        kernel,
        in_specs=[vmem] * len(dense) + [pl.BlockSpec(memory_space=pl.ANY)],
        out_specs=vmem,
        out_shape=jax.ShapeDtypeStruct(shape, BF),
        scratch_shapes=[
            pltpu.VMEM((4, 2, 2, reps, slab, width), BF),
            pltpu.SemaphoreType.DMA((4, 2, reps)),
        ],
        compiler_params=pltpu.CompilerParams(vmem_limit_bytes=60 * MIB),
        cost_estimate=pl.CostEstimate(
            flops=8 * shape[-2] * width * width, bytes_accessed=8 * width * width, transcendentals=0
        ),
        name=name,
    )(*dense, zero)


def grad_kernel(x_ref, *refs):
    pieces, csum_ref, (o_ref, ctl_ref, sum_ref, sems) = refs[:4], refs[4], refs[5:]
    rows = pieces[0].shape[0]
    copies = [pltpu.make_async_copy(csum_ref, sum_ref, sems.at[4])]
    for step, piece in enumerate(pieces):
        start = pl.multiple_of(lax.rem(x_ref[0] + 4 - step, 4) * rows, rows)
        copies.append(pltpu.make_async_copy(piece, ctl_ref.at[pl.ds(start, rows), :], sems.at[step]))
    for copy in copies:
        copy.start()
    for copy in copies:
        copy.wait()
    o_ref[...] = lax.dot_general(
        ctl_ref[...],
        sum_ref[...].reshape(ctl_ref.shape),
        (((0,), (0,)), ((), ())),
        preferred_element_type=F32,
    ).astype(BF)


def grad_partial(x, ctl, csum):
    blocks, rows, width = csum.shape
    return pl.pallas_call(
        grad_kernel,
        in_specs=[pl.BlockSpec(memory_space=pltpu.SMEM)]
        + [pl.BlockSpec(memory_space=pl.ANY)] * 5,
        out_specs=pl.BlockSpec(memory_space=pltpu.VMEM),
        out_shape=jax.ShapeDtypeStruct((width, width), BF),
        scratch_shapes=[
            pltpu.VMEM((blocks * rows, width), BF),
            pltpu.VMEM(csum.shape, BF),
            pltpu.SemaphoreType.DMA((5,)),
        ],
        compiler_params=pltpu.CompilerParams(vmem_limit_bytes=40 * MIB),
        cost_estimate=pl.CostEstimate(
            flops=8 * rows * width * width, bytes_accessed=18 * rows * width, transcendentals=0
        ),
        name="grad_partial",
    )(x, *ctl, csum)


def pick(blocks, index):
    return lax.dynamic_index_in_dim(blocks, index, 0, keepdims=False)


def ordered(blocks, source):
    result = []
    for j in range(len(blocks)):
        block = blocks[0]
        for step in range(1, len(blocks)):
            block = jnp.where(source(step) == j, blocks[step], block)
        result.append(block)
    return result


def shards(hidden, queries_keys, values, text_len, timestep, gate_table, w_out, w_zero, cotangent):
    g = lax.axis_index("grp")
    x = lax.axis_index("x")
    core = lax.axis_index("core")
    rep = lax.axis_index("rep")
    zl = lax.axis_index("zl")
    is_control = g == 0
    n_grp, n_x, n_rep = SIZES["grp"], SIZES["x"], SIZES["rep"]
    tok, width = hidden.shape[2], w_zero.shape[1]

    def source(step):
        return (g - step) % n_grp

    w_sel = jnp.where(is_control, w_out[0], w_out[1])
    weight = lax.all_gather(w_sel, ("x", "core", "rep")).reshape(8, n_rep, *w_sel.shape)

    pair = queries_keys[0, 0].reshape(tok, 2, H, HEAD).transpose(2, 1, 0, 3)
    vals = values[0, 0].reshape(tok, 1, H, HEAD).transpose(2, 1, 0, 3)
    qkv = jnp.concatenate([pair, vals], axis=1)

    qkv = lax.all_to_all(qkv, SEQ, split_axis=0, concat_axis=0, tiled=True)
    turn = [(i * n_grp + j, j * n_grp + i) for i in range(n_x) for j in range(n_grp)]
    slab = w_zero.shape[0] // n_rep
    zero_slab = lax.dynamic_slice_in_dim(w_zero, rep * slab, slab, axis=0)
    zero_slab = lax.ppermute(zero_slab, ("grp", "x"), turn)

    def cot_block(index):
        return lax.dynamic_slice_in_dim(cotangent[0, 0], index * width, width, axis=1)

    cots = [cot_block(g)] + [
        shift(cot_block((g + step) % n_grp), "grp", step) for step in range(1, n_grp)
    ]
    csum = sum(jnp.where(source(step) == 0, 0.0, cots[step].astype(F32)) for step in range(n_grp))
    own_cot = sum(jnp.where(source(step) == 0, cots[step], 0) for step in range(n_grp))
    csum = csum.astype(BF)
    slab_other = shift(zero_slab, "zl", 1)
    attn, csum, own_cot, zero_slab, slab_other = gate(
        attend(qkv, text_len), csum, own_cot, zero_slab, slab_other
    )
    csums = [csum] + [shift(csum, "grp", step) for step in range(1, n_grp)]
    slabs = jnp.stack(
        [jnp.where(zl == 0, zero_slab, slab_other), jnp.where(zl == 0, slab_other, zero_slab)]
    )
    zero_rows = lax.all_gather(slabs, ("x", "core", "rep"))

    parts = attn.reshape(n_x, 2, 2, tok, HEAD).transpose(0, 2, 1, 3, 4).reshape(8, 2 * tok, HEAD)
    heads = lax.all_to_all(parts, ("x", "core"), split_axis=0, concat_axis=0, tiled=True)
    level = lax.dynamic_slice_in_dim(gate_table, timestep[0, 0], 1, axis=0)

    def finish(first, own, other):
        at = slice(first * width, first * width + own.shape[1])
        proj = own + other.astype(F32)
        return (hidden[0, 0][:, at].astype(F32) + level[:, at] * proj).astype(BF)

    own_b, other_b = project(zl.reshape(1), heads, weight, 2, 2)
    heads, other_b = gate(heads, other_b)
    other_b = shift(other_b, "zl", 1)
    own_a, other_a = project(zl.reshape(1), heads, weight, 0, 2)
    other_a, csums = gate(other_a, csums)
    other_a = shift(other_a, "zl", 1)
    csum_all = jnp.stack(ordered(csums, source))
    csum_x = lax.all_to_all(csum_all, "x", split_axis=0, concat_axis=0, tiled=True)
    (out_b,) = gate(finish(2, own_b, other_b))
    parts = [send(out_b[:, :width], "grp", [(0, 2)]), send(out_b[:, width:], "grp", [(0, 3)])]
    out_a = finish(0, own_a, other_a)
    parts = [send(out_a[:, width:], "grp", [(0, 1)])] + parts
    out = jnp.concatenate([out_a, out_b], axis=1)
    control = out_a[:, :width]
    for j in range(1, n_grp):
        control = jnp.where(g == j, parts[j - 1], control)
    zero_rows = zero_rows.reshape(n_x, 2, n_rep, 2, slab, width)
    control, zero_rows, csum_x = gate(control, zero_rows, csum_x)

    resid = with_zero(resid_kernel, [control], zero_rows, (n_grp, tok, width), "residual")
    resid, control = gate(resid, control)
    resid = lax.all_to_all(resid, "grp", split_axis=0, concat_axis=0, tiled=True)
    mine_r = jnp.sum(resid.astype(F32), axis=0).astype(BF)
    ctl_x = ring_gather(control, "x")
    partial = grad_partial(x.reshape(1), ctl_x, csum_x)
    rows = width // 16
    partial = partial.reshape(2, 2, n_rep * rows, width).transpose(1, 0, 2, 3)
    mine = pick(partial, core).astype(F32)
    got = shift(pick(partial, 1 - core), "core", 1)
    halves = (mine + got.astype(F32)).astype(BF).reshape(2 * n_rep, rows, width)
    halves, csum_all = gate(halves, csum_all)
    ctrl_grad = with_zero(
        term_kernel, [csum_all, own_cot], zero_rows, (tok, width), "control_gradient"
    )
    halves, mine_r, ctrl_grad = gate(halves, mine_r, ctrl_grad)
    halves = lax.all_to_all(halves, ("zl", "rep"), split_axis=0, concat_axis=0, tiled=True)
    grad = jnp.sum(halves.astype(F32), axis=0).astype(BF)
    grad_zero = lax.ppermute(grad, ("grp", "x"), turn).astype(F32)
    blocks = [mine_r]
    for step in range(1, n_grp):
        pairs = [(i, (i + step) % n_grp) for i in range(n_grp) if (i + step) % n_grp]
        blocks.append(send(mine_r, "grp", pairs))
    resid_all = jnp.concatenate(ordered(blocks, source), axis=1)
    final = jnp.where(is_control, out, (out.astype(F32) + resid_all.astype(F32)).astype(BF))

    return (final[None, None], ctrl_grad[None], grad_zero)


def solution(mesh):
    split = Mesh(mesh.devices.reshape(4, 4, 2, 2, 4), ("grp", "x", "zl", "core", "rep"))
    placed = (
        P("rep", "grp", SEQ, None),
        P("rep", "grp", SEQ, None, None),
        P("rep", "grp", SEQ, None),
        P("rep", "grp"),
        P("rep", "grp"),
        P(),
        P(None, SEQ, "rep"),
        P(SEQ, "grp"),
        P("rep", "grp", SEQ, None),
    )
    return jax.shard_map(
        shards,
        mesh=split,
        in_specs=placed,
        out_specs=(P("rep", "grp", SEQ, None), P("rep", SEQ, "grp"), P((*SEQ, "rep"), "grp")),
        check_vma=False,
    )
```

```python
import functools
import math

import jax
import jax.numpy as jnp
from jax import lax
from jax.experimental import pallas as pl
from jax.experimental.pallas import tpu as pltpu
from jax.sharding import Mesh, PartitionSpec as P

H = 16
HEAD = 128
SIZES = {"grp": 4, "x": 4, "zl": 2, "core": 2, "rep": 4}
SEQ = ("x", "zl", "core")
BF = jnp.bfloat16
F32 = jnp.float32
MIB = 1 << 20


def send(value, axis, pairs):
    return lax.ppermute(value, axis, pairs)


def shift(value, axis, step):
    n = SIZES[axis]
    return lax.ppermute(value, axis, [(i, (i + step) % n) for i in range(n)])


def attend_kernel(tlen_ref, q_ref, k_ref, v_ref, o_ref, wide_ref, *, text_slots, scale):
    @pl.when(pl.program_id(0) == 0)
    def _():
        length = wide_ref.shape[0]
        wide_ref[:, :HEAD] = v_ref[...].reshape(length, HEAD)
        wide_ref[:, HEAD:] = jnp.ones((length, HEAD), BF)

    rows = o_ref.shape[0]
    q = q_ref[...].reshape(rows, HEAD)
    length = wide_ref.shape[0]
    k = k_ref[...].reshape(length, HEAD)
    s = lax.dot_general(q, k, (((1,), (1,)), ((), ())), preferred_element_type=F32)
    place = lax.broadcasted_iota(jnp.int32, (rows, text_slots), 1)
    head = jnp.where(place < tlen_ref[0, 0], s[:, :text_slots], -jnp.inf)
    tail = s[:, text_slots:]
    top = jnp.maximum(
        jnp.max(head, axis=1, keepdims=True), jnp.max(tail, axis=1, keepdims=True)
    )
    factor = scale * math.log2(math.e)
    p_head = jnp.exp2((head - top) * factor).astype(BF)
    p_tail = jnp.exp2((tail - top) * factor).astype(BF)
    both = jnp.dot(p_head, wide_ref[:text_slots, :], preferred_element_type=F32) + jnp.dot(
        p_tail, wide_ref[text_slots:, :], preferred_element_type=F32
    )
    o_ref[...] = (both[:, :HEAD] / both[:, HEAD:]).astype(BF)


def attend(qkv, tlen):
    blocks, _, per, _ = qkv.shape
    length = blocks * per
    q_blocks = 2
    rows = q_blocks * per
    whole = lambda part: pl.BlockSpec((blocks, None, per, HEAD), lambda i: (0, part, 0, 0))
    return pl.pallas_call(
        functools.partial(attend_kernel, text_slots=length // 8, scale=HEAD ** -0.5),
        grid=(length // rows,),
        in_specs=[
            pl.BlockSpec(memory_space=pltpu.SMEM),
            pl.BlockSpec((q_blocks, None, per, HEAD), lambda i: (i, 0, 0, 0)),
            whole(1),
            whole(2),
        ],
        out_specs=pl.BlockSpec((rows, HEAD), lambda i: (i, 0)),
        out_shape=jax.ShapeDtypeStruct((length, HEAD), BF),
        scratch_shapes=[pltpu.VMEM((length, 2 * HEAD), BF)],
        compiler_params=pltpu.CompilerParams(vmem_limit_bytes=40 * MIB),
        cost_estimate=pl.CostEstimate(
            flops=6 * length * length * HEAD,
            bytes_accessed=8 * length * HEAD,
            transcendentals=length * length,
        ),
        name="attend",
    )(tlen, qkv, qkv, qkv)


def project_kernel(zl_ref, a_ref, w_ref, own_ref, other_ref, a_held, wide_ref, held, sems, *, first):
    heads, half = held.shape[0], own_ref.shape[0]
    count, _, width = held.shape[1:]
    load = pltpu.make_async_copy(a_ref, a_held, sems.at[heads])
    load.start()
    copies = [
        pltpu.make_async_copy(w_ref.at[h, pl.ds(first, count)], held.at[h], sems.at[h])
        for h in range(heads)
    ]
    for copy in copies:
        copy.start()
    mine = pl.multiple_of(zl_ref[0] * half, half)
    theirs = pl.multiple_of((1 - zl_ref[0]) * half, half)
    load.wait()
    for h in range(heads):
        lanes = slice(h * HEAD, (h + 1) * HEAD)
        wide_ref[:half, lanes] = a_held[h, pl.ds(mine, half), :]
        wide_ref[half:, lanes] = a_held[h, pl.ds(theirs, half), :]
    for copy in copies:
        copy.wait()
    for j in range(count):
        w = held[:, j].reshape(heads * HEAD, width)
        total = jnp.dot(wide_ref[...], w, preferred_element_type=F32)
        lanes = slice(j * width, (j + 1) * width)
        own_ref[:, lanes] = total[:half]
        other_ref[:, lanes] = total[half:].astype(BF)


def project(zl, attn, weight, first, count):
    heads, rows, _ = attn.shape
    _, _, depth, width = weight.shape
    half = rows // 2
    vmem, anywhere = pl.BlockSpec(memory_space=pltpu.VMEM), pl.BlockSpec(memory_space=pl.ANY)
    return pl.pallas_call(
        functools.partial(project_kernel, first=first),
        in_specs=[pl.BlockSpec(memory_space=pltpu.SMEM), anywhere, anywhere],
        out_specs=[vmem, vmem],
        out_shape=[
            jax.ShapeDtypeStruct((half, count * width), F32),
            jax.ShapeDtypeStruct((half, count * width), BF),
        ],
        scratch_shapes=[
            pltpu.VMEM(attn.shape, BF),
            pltpu.VMEM((rows, heads * HEAD), BF),
            pltpu.VMEM((heads, count, depth, width), BF),
            pltpu.SemaphoreType.DMA((heads + 1,)),
        ],
        compiler_params=pltpu.CompilerParams(vmem_limit_bytes=60 * MIB),
        cost_estimate=pl.CostEstimate(
            flops=2 * rows * heads * HEAD * count * width,
            bytes_accessed=2 * heads * HEAD * count * width,
            transcendentals=0,
        ),
        name="project",
    )(zl, attn, weight)


def ring_gather(value, axis):
    return [value] + [shift(value, axis, step) for step in range(1, 4)]


def gate(*values):
    return lax.optimization_barrier(values)


def fetch_zero(zero_ref, held, sems):
    copies = []
    for x in range(4):
        for core in range(2):
            for rep in range(4):
                target = held.at[x, :, core, rep]
                copies.append(pltpu.make_async_copy(zero_ref.at[x, core, rep], target, sems.at[x, core, rep]))
    for copy in copies:
        copy.start()
    return copies


def block_of(held, copies, j):
    for copy in copies[8 * j : 8 * (j + 1)]:
        copy.wait()
    width = held.shape[-1]
    return held[j].reshape(width, width)


def resid_kernel(ctl_ref, zero_ref, o_ref, held, sems):
    copies = fetch_zero(zero_ref, held, sems)
    for j in range(4):
        w = block_of(held, copies, j)
        o_ref[j] = jnp.dot(ctl_ref[...], w, preferred_element_type=F32).astype(BF)


def term_kernel(csum_ref, cot_ref, zero_ref, o_ref, held, sems):
    copies = fetch_zero(zero_ref, held, sems)
    total = 0.0
    for j in range(4):
        term = lax.dot_general(
            csum_ref[j],
            block_of(held, copies, j),
            (((1,), (1,)), ((), ())),
            preferred_element_type=F32,
        )
        if j == 0:
            term = term + cot_ref[...].astype(F32)
        total = total + term.astype(BF).astype(F32)
    o_ref[...] = total.astype(BF)


def with_zero(kernel, dense, zero, shape, name):
    _, _, reps, _, slab, width = zero.shape
    vmem = pl.BlockSpec(memory_space=pltpu.VMEM)
    return pl.pallas_call(
        kernel,
        in_specs=[vmem] * len(dense) + [pl.BlockSpec(memory_space=pl.ANY)],
        out_specs=vmem,
        out_shape=jax.ShapeDtypeStruct(shape, BF),
        scratch_shapes=[
            pltpu.VMEM((4, 2, 2, reps, slab, width), BF),
            pltpu.SemaphoreType.DMA((4, 2, reps)),
        ],
        compiler_params=pltpu.CompilerParams(vmem_limit_bytes=60 * MIB),
        cost_estimate=pl.CostEstimate(
            flops=8 * shape[-2] * width * width, bytes_accessed=8 * width * width, transcendentals=0
        ),
        name=name,
    )(*dense, zero)


def grad_kernel(x_ref, *refs):
    pieces, csum_ref, (o_ref, ctl_ref, sum_ref, sems) = refs[:4], refs[4], refs[5:]
    rows = pieces[0].shape[0]
    copies = [pltpu.make_async_copy(csum_ref, sum_ref, sems.at[4])]
    for step, piece in enumerate(pieces):
        start = pl.multiple_of(lax.rem(x_ref[0] + 4 - step, 4) * rows, rows)
        copies.append(pltpu.make_async_copy(piece, ctl_ref.at[pl.ds(start, rows), :], sems.at[step]))
    for copy in copies:
        copy.start()
    for copy in copies:
        copy.wait()
    o_ref[...] = lax.dot_general(
        ctl_ref[...],
        sum_ref[...].reshape(ctl_ref.shape),
        (((0,), (0,)), ((), ())),
        preferred_element_type=F32,
    ).astype(BF)


def grad_partial(x, ctl, csum):
    blocks, rows, width = csum.shape
    return pl.pallas_call(
        grad_kernel,
        in_specs=[pl.BlockSpec(memory_space=pltpu.SMEM)]
        + [pl.BlockSpec(memory_space=pl.ANY)] * 5,
        out_specs=pl.BlockSpec(memory_space=pltpu.VMEM),
        out_shape=jax.ShapeDtypeStruct((width, width), BF),
        scratch_shapes=[
            pltpu.VMEM((blocks * rows, width), BF),
            pltpu.VMEM(csum.shape, BF),
            pltpu.SemaphoreType.DMA((5,)),
        ],
        compiler_params=pltpu.CompilerParams(vmem_limit_bytes=40 * MIB),
        cost_estimate=pl.CostEstimate(
            flops=8 * rows * width * width, bytes_accessed=18 * rows * width, transcendentals=0
        ),
        name="grad_partial",
    )(x, *ctl, csum)


def pick(blocks, index):
    return lax.dynamic_index_in_dim(blocks, index, 0, keepdims=False)


def ordered(blocks, source):
    result = []
    for j in range(len(blocks)):
        block = blocks[0]
        for step in range(1, len(blocks)):
            block = jnp.where(source(step) == j, blocks[step], block)
        result.append(block)
    return result


def shards(hidden, queries_keys, values, text_len, timestep, gate_table, w_out, w_zero, cotangent):
    g = lax.axis_index("grp")
    x = lax.axis_index("x")
    core = lax.axis_index("core")
    rep = lax.axis_index("rep")
    zl = lax.axis_index("zl")
    is_control = g == 0
    n_grp, n_x, n_rep = SIZES["grp"], SIZES["x"], SIZES["rep"]
    tok, width = hidden.shape[2], w_zero.shape[1]

    def source(step):
        return (g - step) % n_grp

    pair = queries_keys[0, 0].reshape(tok, 2, H, HEAD).transpose(2, 1, 0, 3)
    vals = values[0, 0].reshape(tok, 1, H, HEAD).transpose(2, 1, 0, 3)
    qkv, w_both = gate(jnp.concatenate([pair, vals], axis=1), w_out)
    w_sel = jnp.where(is_control, w_both[0], w_both[1])
    weight = lax.all_gather(w_sel, ("x", "core", "rep")).reshape(8, n_rep, *w_sel.shape)

    qkv = lax.all_to_all(qkv, SEQ, split_axis=0, concat_axis=0, tiled=True)
    turn = [(i * n_grp + j, j * n_grp + i) for i in range(n_x) for j in range(n_grp)]
    slab = w_zero.shape[0] // n_rep
    zero_slab = lax.dynamic_slice_in_dim(w_zero, rep * slab, slab, axis=0)
    zero_slab = lax.ppermute(zero_slab, ("grp", "x"), turn)

    qkv, zero_slab, cot = gate(qkv, zero_slab, cotangent[0, 0])

    def cot_block(index):
        return lax.dynamic_slice_in_dim(cot, index * width, width, axis=1)

    cots = [cot_block(g)] + [
        shift(cot_block((g + step) % n_grp), "grp", step) for step in range(1, n_grp)
    ]
    slab_other = shift(zero_slab, "zl", 1)
    attn, zero_slab, slab_other, cots = gate(
        attend(qkv, text_len), zero_slab, slab_other, cots
    )
    slabs = jnp.stack(
        [jnp.where(zl == 0, zero_slab, slab_other), jnp.where(zl == 0, slab_other, zero_slab)]
    )
    zero_rows = lax.all_gather(slabs, ("x", "core", "rep"))

    parts = attn.reshape(n_x, 2, 2, tok, HEAD).transpose(0, 2, 1, 3, 4).reshape(8, 2 * tok, HEAD)
    heads = lax.all_to_all(parts, ("x", "core"), split_axis=0, concat_axis=0, tiled=True)
    csum = sum(jnp.where(source(step) == 0, 0.0, cots[step].astype(F32)) for step in range(n_grp))
    own_cot = sum(jnp.where(source(step) == 0, cots[step], 0) for step in range(n_grp))
    csum = csum.astype(BF)
    csums = [csum] + [shift(csum, "grp", step) for step in range(1, n_grp)]
    level = lax.dynamic_slice_in_dim(gate_table, timestep[0, 0], 1, axis=0)

    def finish(first, own, other):
        at = slice(first * width, first * width + own.shape[1])
        proj = own + other.astype(F32)
        return (hidden[0, 0][:, at].astype(F32) + level[:, at] * proj).astype(BF)

    own_b, other_b = project(zl.reshape(1), heads, weight, 2, 2)
    heads, other_b = gate(heads, other_b)
    other_b = shift(other_b, "zl", 1)
    own_a, other_a = project(zl.reshape(1), heads, weight, 0, 2)
    other_a, csums = gate(other_a, csums)
    other_a = shift(other_a, "zl", 1)
    (out_b,) = gate(finish(2, own_b, other_b))
    parts = [send(out_b[:, :width], "grp", [(0, 2)]), send(out_b[:, width:], "grp", [(0, 3)])]
    out_a = finish(0, own_a, other_a)
    parts = [send(out_a[:, width:], "grp", [(0, 1)])] + parts
    out = jnp.concatenate([out_a, out_b], axis=1)
    csum_all = jnp.stack(ordered(csums, source))
    csum_x = lax.all_to_all(csum_all, "x", split_axis=0, concat_axis=0, tiled=True)
    control = out_a[:, :width]
    for j in range(1, n_grp):
        control = jnp.where(g == j, parts[j - 1], control)
    zero_rows = zero_rows.reshape(n_x, 2, n_rep, 2, slab, width)
    control, zero_rows, csum_x = gate(control, zero_rows, csum_x)

    resid = with_zero(resid_kernel, [control], zero_rows, (n_grp, tok, width), "residual")
    resid, control = gate(resid, control)
    resid = lax.all_to_all(resid, "grp", split_axis=0, concat_axis=0, tiled=True)
    mine_r = jnp.sum(resid.astype(F32), axis=0).astype(BF)
    ctl_x = ring_gather(control, "x")
    partial = grad_partial(x.reshape(1), ctl_x, csum_x)
    rows = width // 16
    partial = partial.reshape(2, 2, n_rep * rows, width).transpose(1, 0, 2, 3)
    mine = pick(partial, core).astype(F32)
    got = shift(pick(partial, 1 - core), "core", 1)
    halves = (mine + got.astype(F32)).astype(BF).reshape(2 * n_rep, rows, width)
    halves, csum_all = gate(halves, csum_all)
    ctrl_grad = with_zero(
        term_kernel, [csum_all, own_cot], zero_rows, (tok, width), "control_gradient"
    )
    halves, mine_r, ctrl_grad = gate(halves, mine_r, ctrl_grad)
    halves = lax.all_to_all(halves, ("zl", "rep"), split_axis=0, concat_axis=0, tiled=True)
    grad = jnp.sum(halves.astype(F32), axis=0).astype(BF)
    grad_zero = lax.ppermute(grad, ("grp", "x"), turn).astype(F32)
    blocks = [mine_r]
    for step in range(1, n_grp):
        pairs = [(i, (i + step) % n_grp) for i in range(n_grp) if (i + step) % n_grp]
        blocks.append(send(mine_r, "grp", pairs))
    blocks, grad_zero = gate(blocks, grad_zero)
    resid_all = jnp.concatenate(ordered(blocks, source), axis=1)
    final = jnp.where(is_control, out, (out.astype(F32) + resid_all.astype(F32)).astype(BF))

    return (final[None, None], ctrl_grad[None], grad_zero)


def solution(mesh):
    split = Mesh(mesh.devices.reshape(4, 4, 2, 2, 4), ("grp", "x", "zl", "core", "rep"))
    placed = (
        P("rep", "grp", SEQ, None),
        P("rep", "grp", SEQ, None, None),
        P("rep", "grp", SEQ, None),
        P("rep", "grp"),
        P("rep", "grp"),
        P(),
        P(None, SEQ, "rep"),
        P(SEQ, "grp"),
        P("rep", "grp", SEQ, None),
    )
    return jax.shard_map(
        shards,
        mesh=split,
        in_specs=placed,
        out_specs=(P("rep", "grp", SEQ, None), P("rep", SEQ, "grp"), P((*SEQ, "rep"), "grp")),
        check_vma=False,
    )
```

```python
import functools
import math

import jax
import jax.numpy as jnp
from jax import lax
from jax.experimental import pallas as pl
from jax.experimental.pallas import tpu as pltpu
from jax.sharding import Mesh, PartitionSpec as P

H = 16
HEAD = 128
SIZES = {"grp": 4, "x": 4, "zl": 2, "core": 2, "rep": 4}
SEQ = ("x", "zl", "core")
BF = jnp.bfloat16
F32 = jnp.float32
MIB = 1 << 20


def send(value, axis, pairs):
    return lax.ppermute(value, axis, pairs)


def shift(value, axis, step):
    n = SIZES[axis]
    return lax.ppermute(value, axis, [(i, (i + step) % n) for i in range(n)])


def attend_kernel(tlen_ref, q_ref, k_ref, v_ref, o_ref, wide_ref, *, text_slots, scale):
    @pl.when(pl.program_id(0) == 0)
    def _():
        length = wide_ref.shape[0]
        wide_ref[:, :HEAD] = v_ref[...].reshape(length, HEAD)
        wide_ref[:, HEAD:] = jnp.ones((length, HEAD), BF)

    length = wide_ref.shape[0]
    k = k_ref[...].reshape(length, HEAD)
    factor = scale * math.log2(math.e)
    blocks, rows, _ = q_ref.shape
    for at in range(0, blocks, 2):
        q = q_ref[at : at + 2].reshape(2 * rows, HEAD)
        s = lax.dot_general(q, k, (((1,), (1,)), ((), ())), preferred_element_type=F32)
        place = lax.broadcasted_iota(jnp.int32, (2 * rows, text_slots), 1)
        head = jnp.where(place < tlen_ref[0, 0], s[:, :text_slots], -jnp.inf)
        tail = s[:, text_slots:]
        top = jnp.maximum(
            jnp.max(head, axis=1, keepdims=True), jnp.max(tail, axis=1, keepdims=True)
        )
        p_head = jnp.exp2((head - top) * factor).astype(BF)
        p_tail = jnp.exp2((tail - top) * factor).astype(BF)
        both = jnp.dot(p_head, wide_ref[:text_slots, :], preferred_element_type=F32) + jnp.dot(
            p_tail, wide_ref[text_slots:, :], preferred_element_type=F32
        )
        result = (both[:, :HEAD] / both[:, HEAD:]).astype(BF)
        o_ref[at // 4, 0, at % 4 // 2] = result[:rows]
        o_ref[at // 4, 1, at % 4 // 2] = result[rows:]


def attend(qkv, tlen):
    blocks, _, per, _ = qkv.shape
    length = blocks * per
    q_blocks = 8
    rows = q_blocks * per
    whole = lambda part: pl.BlockSpec((blocks, None, per, HEAD), lambda i: (0, part, 0, 0))
    return pl.pallas_call(
        functools.partial(attend_kernel, text_slots=length // 8, scale=HEAD ** -0.5),
        grid=(length // rows,),
        in_specs=[
            pl.BlockSpec(memory_space=pltpu.SMEM),
            pl.BlockSpec((q_blocks, None, per, HEAD), lambda i: (i, 0, 0, 0)),
            whole(1),
            whole(2),
        ],
        out_specs=pl.BlockSpec((q_blocks // 4, 2, 2, per, HEAD), lambda i: (i, 0, 0, 0, 0)),
        out_shape=jax.ShapeDtypeStruct((blocks // 4, 2, 2, per, HEAD), BF),
        scratch_shapes=[pltpu.VMEM((length, 2 * HEAD), BF)],
        compiler_params=pltpu.CompilerParams(vmem_limit_bytes=56 * MIB),
        cost_estimate=pl.CostEstimate(
            flops=6 * length * length * HEAD,
            bytes_accessed=8 * length * HEAD,
            transcendentals=length * length,
        ),
        name="attend",
    )(tlen, qkv, qkv, qkv)


def project_kernel(zl_ref, a_ref, w_ref, own_ref, other_ref, a_held, wide_ref, held, sems, *, first):
    heads, half = held.shape[0], own_ref.shape[0]
    count, _, width = held.shape[1:]
    load = pltpu.make_async_copy(a_ref, a_held, sems.at[heads])
    load.start()
    copies = [
        pltpu.make_async_copy(w_ref.at[h, pl.ds(first, count)], held.at[h], sems.at[h])
        for h in range(heads)
    ]
    for copy in copies:
        copy.start()
    mine = pl.multiple_of(zl_ref[0] * half, half)
    theirs = pl.multiple_of((1 - zl_ref[0]) * half, half)
    load.wait()
    for h in range(heads):
        lanes = slice(h * HEAD, (h + 1) * HEAD)
        wide_ref[:half, lanes] = a_held[h, pl.ds(mine, half), :]
        wide_ref[half:, lanes] = a_held[h, pl.ds(theirs, half), :]
    for copy in copies:
        copy.wait()
    for j in range(count):
        w = held[:, j].reshape(heads * HEAD, width)
        total = jnp.dot(wide_ref[...], w, preferred_element_type=F32)
        lanes = slice(j * width, (j + 1) * width)
        own_ref[:, lanes] = total[:half]
        other_ref[:, lanes] = total[half:].astype(BF)


def project(zl, attn, weight, first, count):
    heads, rows, _ = attn.shape
    _, _, depth, width = weight.shape
    half = rows // 2
    vmem, anywhere = pl.BlockSpec(memory_space=pltpu.VMEM), pl.BlockSpec(memory_space=pl.ANY)
    return pl.pallas_call(
        functools.partial(project_kernel, first=first),
        in_specs=[pl.BlockSpec(memory_space=pltpu.SMEM), anywhere, anywhere],
        out_specs=[vmem, vmem],
        out_shape=[
            jax.ShapeDtypeStruct((half, count * width), F32),
            jax.ShapeDtypeStruct((half, count * width), BF),
        ],
        scratch_shapes=[
            pltpu.VMEM(attn.shape, BF),
            pltpu.VMEM((rows, heads * HEAD), BF),
            pltpu.VMEM((heads, count, depth, width), BF),
            pltpu.SemaphoreType.DMA((heads + 1,)),
        ],
        compiler_params=pltpu.CompilerParams(vmem_limit_bytes=60 * MIB),
        cost_estimate=pl.CostEstimate(
            flops=2 * rows * heads * HEAD * count * width,
            bytes_accessed=2 * heads * HEAD * count * width,
            transcendentals=0,
        ),
        name="project",
    )(zl, attn, weight)


def ring_gather(value, axis):
    return [value] + [shift(value, axis, step) for step in range(1, 4)]


def gate(*values):
    return lax.optimization_barrier(values)


def fetch_zero(zero_ref, held, sems):
    copies = []
    for x in range(4):
        for core in range(2):
            for rep in range(4):
                target = held.at[x, :, core, rep]
                copies.append(pltpu.make_async_copy(zero_ref.at[x, core, rep], target, sems.at[x, core, rep]))
    for copy in copies:
        copy.start()
    return copies


def block_of(held, copies, j):
    for copy in copies[8 * j : 8 * (j + 1)]:
        copy.wait()
    width = held.shape[-1]
    return held[j].reshape(width, width)


def term_kernel(csum_ref, cot_ref, zero_ref, o_ref, held, sems):
    copies = fetch_zero(zero_ref, held, sems)
    total = 0.0
    for j in range(4):
        term = lax.dot_general(
            csum_ref[j],
            block_of(held, copies, j),
            (((1,), (1,)), ((), ())),
            preferred_element_type=F32,
        )
        if j == 0:
            term = term + cot_ref[...].astype(F32)
        total = total + term.astype(BF).astype(F32)
    o_ref[...] = total.astype(BF)


def with_zero(kernel, dense, zero, shape, name):
    _, _, reps, _, slab, width = zero.shape
    vmem = pl.BlockSpec(memory_space=pltpu.VMEM)
    return pl.pallas_call(
        kernel,
        in_specs=[vmem] * len(dense) + [pl.BlockSpec(memory_space=pl.ANY)],
        out_specs=vmem,
        out_shape=jax.ShapeDtypeStruct(shape, BF),
        scratch_shapes=[
            pltpu.VMEM((4, 2, 2, reps, slab, width), BF),
            pltpu.SemaphoreType.DMA((4, 2, reps)),
        ],
        compiler_params=pltpu.CompilerParams(vmem_limit_bytes=60 * MIB),
        cost_estimate=pl.CostEstimate(
            flops=8 * shape[-2] * width * width, bytes_accessed=8 * width * width, transcendentals=0
        ),
        name=name,
    )(*dense, zero)


def grad_kernel(x_ref, *refs):
    pieces, csum_ref, (o_ref, ctl_ref, sum_ref, sems) = refs[:4], refs[4], refs[5:]
    rows = pieces[0].shape[0]
    copies = [pltpu.make_async_copy(csum_ref, sum_ref, sems.at[4])]
    for step, piece in enumerate(pieces):
        start = pl.multiple_of(lax.rem(x_ref[0] + 4 - step, 4) * rows, rows)
        copies.append(pltpu.make_async_copy(piece, ctl_ref.at[pl.ds(start, rows), :], sems.at[step]))
    for copy in copies:
        copy.start()
    for copy in copies:
        copy.wait()
    o_ref[...] = lax.dot_general(
        ctl_ref[...],
        sum_ref[...].reshape(ctl_ref.shape),
        (((0,), (0,)), ((), ())),
        preferred_element_type=F32,
    ).astype(BF)


def grad_partial(x, ctl, csum):
    blocks, rows, width = csum.shape
    return pl.pallas_call(
        grad_kernel,
        in_specs=[pl.BlockSpec(memory_space=pltpu.SMEM)]
        + [pl.BlockSpec(memory_space=pl.ANY)] * 5,
        out_specs=pl.BlockSpec(memory_space=pltpu.VMEM),
        out_shape=jax.ShapeDtypeStruct((width, width), BF),
        scratch_shapes=[
            pltpu.VMEM((blocks * rows, width), BF),
            pltpu.VMEM(csum.shape, BF),
            pltpu.SemaphoreType.DMA((5,)),
        ],
        compiler_params=pltpu.CompilerParams(vmem_limit_bytes=40 * MIB),
        cost_estimate=pl.CostEstimate(
            flops=8 * rows * width * width, bytes_accessed=18 * rows * width, transcendentals=0
        ),
        name="grad_partial",
    )(x, *ctl, csum)


def pick(blocks, index):
    return lax.dynamic_index_in_dim(blocks, index, 0, keepdims=False)


def ordered(blocks, source):
    result = []
    for j in range(len(blocks)):
        block = blocks[0]
        for step in range(1, len(blocks)):
            block = jnp.where(source(step) == j, blocks[step], block)
        result.append(block)
    return result


def shards(hidden, queries_keys, values, text_len, timestep, gate_table, w_out, w_zero, cotangent):
    g = lax.axis_index("grp")
    x = lax.axis_index("x")
    core = lax.axis_index("core")
    rep = lax.axis_index("rep")
    zl = lax.axis_index("zl")
    is_control = g == 0
    n_grp, n_x, n_rep = SIZES["grp"], SIZES["x"], SIZES["rep"]
    tok, width = hidden.shape[2], w_zero.shape[1]

    def source(step):
        return (g - step) % n_grp

    pair = queries_keys[0, 0].reshape(tok, 2, H, HEAD).transpose(2, 1, 0, 3)
    vals = values[0, 0].reshape(tok, 1, H, HEAD).transpose(2, 1, 0, 3)
    qkv, w_both = gate(jnp.concatenate([pair, vals], axis=1), w_out)
    w_sel = jnp.where(is_control, w_both[0], w_both[1])
    weight = lax.all_gather(w_sel, ("x", "core", "rep")).reshape(8, n_rep, *w_sel.shape)

    qkv = lax.all_to_all(qkv, SEQ, split_axis=0, concat_axis=0, tiled=True)
    turn = [(i * n_grp + j, j * n_grp + i) for i in range(n_x) for j in range(n_grp)]
    slab = w_zero.shape[0] // n_rep
    zero_slab = lax.dynamic_slice_in_dim(w_zero, rep * slab, slab, axis=0)
    zero_slab = lax.ppermute(zero_slab, ("grp", "x"), turn)

    slab_other = shift(zero_slab, "zl", 1)
    slabs = jnp.stack(
        [jnp.where(zl == 0, zero_slab, slab_other), jnp.where(zl == 0, slab_other, zero_slab)]
    )
    qkv, slabs, cot = gate(qkv, slabs, cotangent[0, 0])

    def cot_block(index):
        return lax.dynamic_slice_in_dim(cot, index * width, width, axis=1)

    cots = [cot_block(g)] + [
        shift(cot_block((g + step) % n_grp), "grp", step) for step in range(1, n_grp)
    ]
    attn, slabs, cots = gate(attend(qkv, text_len), slabs, cots)
    zero_rows = lax.all_gather(slabs, ("x", "core", "rep"))

    heads = lax.all_to_all(attn.reshape(8, 2 * tok, HEAD), ("x", "core"), split_axis=0, concat_axis=0, tiled=True)
    csum = sum(jnp.where(source(step) == 0, 0.0, cots[step].astype(F32)) for step in range(n_grp))
    own_cot = sum(jnp.where(source(step) == 0, cots[step], 0) for step in range(n_grp))
    csum = csum.astype(BF)
    csums = [csum] + [shift(csum, "grp", step) for step in range(1, n_grp)]
    level = lax.dynamic_slice_in_dim(gate_table, timestep[0, 0], 1, axis=0)

    def finish(first, own, other):
        at = slice(first * width, first * width + own.shape[1])
        proj = own + other.astype(F32)
        return (hidden[0, 0][:, at].astype(F32) + level[:, at] * proj).astype(BF)

    own_b, other_b = project(zl.reshape(1), heads, weight, 2, 2)
    heads, other_b = gate(heads, other_b)
    other_b = shift(other_b, "zl", 1)
    own_a, other_a = project(zl.reshape(1), heads, weight, 0, 2)
    other_a, csums = gate(other_a, csums)
    other_a = shift(other_a, "zl", 1)
    (out_b,) = gate(finish(2, own_b, other_b))
    parts = [send(out_b[:, :width], "grp", [(0, 2)]), send(out_b[:, width:], "grp", [(0, 3)])]
    out_a = finish(0, own_a, other_a)
    parts = [send(out_a[:, width:], "grp", [(0, 1)])] + parts
    out = jnp.concatenate([out_a, out_b], axis=1)
    csum_all = jnp.stack(ordered(csums, source))
    csum_x = lax.all_to_all(csum_all, "x", split_axis=0, concat_axis=0, tiled=True)
    control = out_a[:, :width]
    for j in range(1, n_grp):
        control = jnp.where(g == j, parts[j - 1], control)
    zero_rows = zero_rows.reshape(n_x, 2, n_rep, 2, slab, width)
    zero_flat = zero_rows.transpose(0, 3, 1, 2, 4, 5).reshape(n_grp, width, width)
    control, zero_rows, zero_flat, csum_x = gate(control, zero_rows, zero_flat, csum_x)

    resid = jnp.einsum("tr,brc->btc", control, zero_flat, preferred_element_type=F32).astype(BF)
    resid, control = gate(resid, control)
    resid = lax.all_to_all(resid, "grp", split_axis=0, concat_axis=0, tiled=True)
    mine_r = jnp.sum(resid.astype(F32), axis=0).astype(BF)
    ctl_x = ring_gather(control, "x")
    partial = grad_partial(x.reshape(1), ctl_x, csum_x)
    rows = width // 16
    partial = partial.reshape(2, 2, n_rep * rows, width).transpose(1, 0, 2, 3)
    mine = pick(partial, core).astype(F32)
    got = shift(pick(partial, 1 - core), "core", 1)
    halves = (mine + got.astype(F32)).astype(BF).reshape(2 * n_rep, rows, width)
    halves, csum_all = gate(halves, csum_all)
    ctrl_grad = with_zero(
        term_kernel, [csum_all, own_cot], zero_rows, (tok, width), "control_gradient"
    )
    halves, mine_r, ctrl_grad = gate(halves, mine_r, ctrl_grad)
    halves = lax.all_to_all(halves, ("zl", "rep"), split_axis=0, concat_axis=0, tiled=True)
    grad = jnp.sum(halves.astype(F32), axis=0).astype(BF)
    grad_zero = lax.ppermute(grad, ("grp", "x"), turn).astype(F32)
    blocks = [mine_r]
    for step in range(1, n_grp):
        pairs = [(i, (i + step) % n_grp) for i in range(n_grp) if (i + step) % n_grp]
        blocks.append(send(mine_r, "grp", pairs))
    blocks, grad_zero = gate(blocks, grad_zero)
    resid_all = jnp.concatenate(ordered(blocks, source), axis=1)
    final = jnp.where(is_control, out, (out.astype(F32) + resid_all.astype(F32)).astype(BF))

    return (final[None, None], ctrl_grad[None], grad_zero)


def solution(mesh):
    split = Mesh(mesh.devices.reshape(4, 4, 2, 2, 4), ("grp", "x", "zl", "core", "rep"))
    placed = (
        P("rep", "grp", SEQ, None),
        P("rep", "grp", SEQ, None, None),
        P("rep", "grp", SEQ, None),
        P("rep", "grp"),
        P("rep", "grp"),
        P(),
        P(None, SEQ, "rep"),
        P(SEQ, "grp"),
        P("rep", "grp", SEQ, None),
    )
    return jax.shard_map(
        shards,
        mesh=split,
        in_specs=placed,
        out_specs=(P("rep", "grp", SEQ, None), P("rep", SEQ, "grp"), P((*SEQ, "rep"), "grp")),
        check_vma=False,
    )
```

```python
import functools
import math

import jax
import jax.numpy as jnp
from jax import lax
from jax.experimental import pallas as pl
from jax.experimental.pallas import tpu as pltpu
from jax.sharding import Mesh, PartitionSpec as P

H = 16
HEAD = 128
SIZES = {"grp": 4, "x": 4, "zl": 2, "core": 2, "rep": 4}
SEQ = ("x", "zl", "core")
BF = jnp.bfloat16
F32 = jnp.float32
MIB = 1 << 20


def send(value, axis, pairs):
    return lax.ppermute(value, axis, pairs)


def shift(value, axis, step):
    n = SIZES[axis]
    return lax.ppermute(value, axis, [(i, (i + step) % n) for i in range(n)])


def attend_kernel(tlen_ref, q_ref, k_ref, v_ref, o_ref, wide_ref, *, text_slots, scale):
    @pl.when(pl.program_id(0) == 0)
    def _():
        length = wide_ref.shape[0]
        wide_ref[:, :HEAD] = v_ref[...].reshape(length, HEAD)
        wide_ref[:, HEAD:] = jnp.ones((length, HEAD), BF)

    length = wide_ref.shape[0]
    k = k_ref[...].reshape(length, HEAD)
    factor = scale * math.log2(math.e)
    blocks, rows, _ = q_ref.shape
    for at in range(0, blocks, 2):
        q = q_ref[at : at + 2].reshape(2 * rows, HEAD)
        s = lax.dot_general(q, k, (((1,), (1,)), ((), ())), preferred_element_type=F32)
        place = lax.broadcasted_iota(jnp.int32, (2 * rows, text_slots), 1)
        head = jnp.where(place < tlen_ref[0, 0], s[:, :text_slots], -jnp.inf)
        tail = s[:, text_slots:]
        top = jnp.maximum(
            jnp.max(head, axis=1, keepdims=True), jnp.max(tail, axis=1, keepdims=True)
        )
        p_head = jnp.exp2((head - top) * factor).astype(BF)
        p_tail = jnp.exp2((tail - top) * factor).astype(BF)
        both = jnp.dot(p_head, wide_ref[:text_slots, :], preferred_element_type=F32) + jnp.dot(
            p_tail, wide_ref[text_slots:, :], preferred_element_type=F32
        )
        result = (both[:, :HEAD] / both[:, HEAD:]).astype(BF)
        o_ref[at // 4, 0, at % 4 // 2] = result[:rows]
        o_ref[at // 4, 1, at % 4 // 2] = result[rows:]


def attend(qkv, tlen):
    blocks, _, per, _ = qkv.shape
    length = blocks * per
    q_blocks = 8
    rows = q_blocks * per
    whole = lambda part: pl.BlockSpec((blocks, None, per, HEAD), lambda i: (0, part, 0, 0))
    return pl.pallas_call(
        functools.partial(attend_kernel, text_slots=length // 8, scale=HEAD ** -0.5),
        grid=(length // rows,),
        in_specs=[
            pl.BlockSpec(memory_space=pltpu.SMEM),
            pl.BlockSpec((q_blocks, None, per, HEAD), lambda i: (i, 0, 0, 0)),
            whole(1),
            whole(2),
        ],
        out_specs=pl.BlockSpec((q_blocks // 4, 2, 2, per, HEAD), lambda i: (i, 0, 0, 0, 0)),
        out_shape=jax.ShapeDtypeStruct((blocks // 4, 2, 2, per, HEAD), BF),
        scratch_shapes=[pltpu.VMEM((length, 2 * HEAD), BF)],
        compiler_params=pltpu.CompilerParams(vmem_limit_bytes=56 * MIB),
        cost_estimate=pl.CostEstimate(
            flops=6 * length * length * HEAD,
            bytes_accessed=8 * length * HEAD,
            transcendentals=length * length,
        ),
        name="attend",
    )(tlen, qkv, qkv, qkv)


def project_kernel(zl_ref, a_ref, w_ref, own_ref, other_ref, a_held, wide_ref, held, sems, *, first):
    heads, half = held.shape[0], own_ref.shape[0]
    count, _, width = held.shape[1:]
    load = pltpu.make_async_copy(a_ref, a_held, sems.at[heads])
    load.start()
    copies = [
        pltpu.make_async_copy(w_ref.at[h, pl.ds(first, count)], held.at[h], sems.at[h])
        for h in range(heads)
    ]
    for copy in copies:
        copy.start()
    mine = pl.multiple_of(zl_ref[0] * half, half)
    theirs = pl.multiple_of((1 - zl_ref[0]) * half, half)
    load.wait()
    for h in range(heads):
        lanes = slice(h * HEAD, (h + 1) * HEAD)
        wide_ref[:half, lanes] = a_held[h, pl.ds(mine, half), :]
        wide_ref[half:, lanes] = a_held[h, pl.ds(theirs, half), :]
    for copy in copies:
        copy.wait()
    for j in range(count):
        w = held[:, j].reshape(heads * HEAD, width)
        total = jnp.dot(wide_ref[...], w, preferred_element_type=F32)
        lanes = slice(j * width, (j + 1) * width)
        own_ref[:, lanes] = total[:half]
        other_ref[:, lanes] = total[half:].astype(BF)


def project(zl, attn, weight, first, count):
    heads, rows, _ = attn.shape
    _, _, depth, width = weight.shape
    half = rows // 2
    vmem, anywhere = pl.BlockSpec(memory_space=pltpu.VMEM), pl.BlockSpec(memory_space=pl.ANY)
    return pl.pallas_call(
        functools.partial(project_kernel, first=first),
        in_specs=[pl.BlockSpec(memory_space=pltpu.SMEM), anywhere, anywhere],
        out_specs=[vmem, vmem],
        out_shape=[
            jax.ShapeDtypeStruct((half, count * width), F32),
            jax.ShapeDtypeStruct((half, count * width), BF),
        ],
        scratch_shapes=[
            pltpu.VMEM(attn.shape, BF),
            pltpu.VMEM((rows, heads * HEAD), BF),
            pltpu.VMEM((heads, count, depth, width), BF),
            pltpu.SemaphoreType.DMA((heads + 1,)),
        ],
        compiler_params=pltpu.CompilerParams(vmem_limit_bytes=60 * MIB),
        cost_estimate=pl.CostEstimate(
            flops=2 * rows * heads * HEAD * count * width,
            bytes_accessed=2 * heads * HEAD * count * width,
            transcendentals=0,
        ),
        name="project",
    )(zl, attn, weight)


def ring_gather(value, axis):
    return [value] + [shift(value, axis, step) for step in range(1, 4)]


def gate(*values):
    return lax.optimization_barrier(values)


def fetch_zero(zero_ref, held, sems):
    copies = []
    for x in range(4):
        for core in range(2):
            for rep in range(4):
                target = held.at[x, :, core, rep]
                copies.append(pltpu.make_async_copy(zero_ref.at[x, core, rep], target, sems.at[x, core, rep]))
    for copy in copies:
        copy.start()
    return copies


def block_of(held, copies, j):
    for copy in copies[8 * j : 8 * (j + 1)]:
        copy.wait()
    width = held.shape[-1]
    return held[j].reshape(width, width)


def term_kernel(csum_ref, cot_ref, zero_ref, o_ref, held, sems):
    copies = fetch_zero(zero_ref, held, sems)
    total = 0.0
    for j in range(4):
        term = lax.dot_general(
            csum_ref[j],
            block_of(held, copies, j),
            (((1,), (1,)), ((), ())),
            preferred_element_type=F32,
        )
        if j == 0:
            term = term + cot_ref[...].astype(F32)
        total = total + term.astype(BF).astype(F32)
    o_ref[...] = total.astype(BF)


def with_zero(kernel, dense, zero, shape, name):
    _, _, reps, _, slab, width = zero.shape
    vmem = pl.BlockSpec(memory_space=pltpu.VMEM)
    return pl.pallas_call(
        kernel,
        in_specs=[vmem] * len(dense) + [pl.BlockSpec(memory_space=pl.ANY)],
        out_specs=vmem,
        out_shape=jax.ShapeDtypeStruct(shape, BF),
        scratch_shapes=[
            pltpu.VMEM((4, 2, 2, reps, slab, width), BF),
            pltpu.SemaphoreType.DMA((4, 2, reps)),
        ],
        compiler_params=pltpu.CompilerParams(vmem_limit_bytes=60 * MIB),
        cost_estimate=pl.CostEstimate(
            flops=8 * shape[-2] * width * width, bytes_accessed=8 * width * width, transcendentals=0
        ),
        name=name,
    )(*dense, zero)


def grad_kernel(x_ref, *refs):
    pieces, csum_ref, (o_ref, ctl_ref, sum_ref, sems) = refs[:4], refs[4], refs[5:]
    rows = pieces[0].shape[0]
    copies = [pltpu.make_async_copy(csum_ref, sum_ref, sems.at[4])]
    for step, piece in enumerate(pieces):
        start = pl.multiple_of(lax.rem(x_ref[0] + 4 - step, 4) * rows, rows)
        copies.append(pltpu.make_async_copy(piece, ctl_ref.at[pl.ds(start, rows), :], sems.at[step]))
    for copy in copies:
        copy.start()
    for copy in copies:
        copy.wait()
    o_ref[...] = lax.dot_general(
        ctl_ref[...],
        sum_ref[...].reshape(ctl_ref.shape),
        (((0,), (0,)), ((), ())),
        preferred_element_type=F32,
    ).astype(BF)


def grad_partial(x, ctl, csum):
    blocks, rows, width = csum.shape
    return pl.pallas_call(
        grad_kernel,
        in_specs=[pl.BlockSpec(memory_space=pltpu.SMEM)]
        + [pl.BlockSpec(memory_space=pl.ANY)] * 5,
        out_specs=pl.BlockSpec(memory_space=pltpu.VMEM),
        out_shape=jax.ShapeDtypeStruct((width, width), BF),
        scratch_shapes=[
            pltpu.VMEM((blocks * rows, width), BF),
            pltpu.VMEM(csum.shape, BF),
            pltpu.SemaphoreType.DMA((5,)),
        ],
        compiler_params=pltpu.CompilerParams(vmem_limit_bytes=40 * MIB),
        cost_estimate=pl.CostEstimate(
            flops=8 * rows * width * width, bytes_accessed=18 * rows * width, transcendentals=0
        ),
        name="grad_partial",
    )(x, *ctl, csum)


def pick(blocks, index):
    return lax.dynamic_index_in_dim(blocks, index, 0, keepdims=False)


def ordered(blocks, source):
    result = []
    for j in range(len(blocks)):
        block = blocks[0]
        for step in range(1, len(blocks)):
            block = jnp.where(source(step) == j, blocks[step], block)
        result.append(block)
    return result


def shards(hidden, queries_keys, values, text_len, timestep, gate_table, w_out, w_zero, cotangent):
    g = lax.axis_index("grp")
    x = lax.axis_index("x")
    core = lax.axis_index("core")
    rep = lax.axis_index("rep")
    zl = lax.axis_index("zl")
    is_control = g == 0
    n_grp, n_x, n_rep = SIZES["grp"], SIZES["x"], SIZES["rep"]
    tok, width = hidden.shape[2], w_zero.shape[1]

    def source(step):
        return (g - step) % n_grp

    pair = queries_keys[0, 0].reshape(tok, 2, H, HEAD).transpose(2, 1, 0, 3)
    vals = values[0, 0].reshape(tok, 1, H, HEAD).transpose(2, 1, 0, 3)
    qkv, w_both = gate(jnp.concatenate([pair, vals], axis=1), w_out)
    w_sel = jnp.where(is_control, w_both[0], w_both[1])
    weight = lax.all_gather(w_sel, ("x", "core", "rep")).reshape(8, n_rep, *w_sel.shape)

    qkv = lax.all_to_all(qkv, SEQ, split_axis=0, concat_axis=0, tiled=True)
    turn = [(i * n_grp + j, j * n_grp + i) for i in range(n_x) for j in range(n_grp)]
    slab = w_zero.shape[0] // n_rep
    zero_slab = lax.dynamic_slice_in_dim(w_zero, rep * slab, slab, axis=0)
    zero_slab = lax.ppermute(zero_slab, ("grp", "x"), turn)

    slab_other = shift(zero_slab, "zl", 1)
    slabs = jnp.stack(
        [jnp.where(zl == 0, zero_slab, slab_other), jnp.where(zl == 0, slab_other, zero_slab)]
    )
    qkv, slabs, cot = gate(qkv, slabs, cotangent[0, 0])

    def cot_block(index):
        return lax.dynamic_slice_in_dim(cot, index * width, width, axis=1)

    cots = [cot_block(g)] + [
        shift(cot_block((g + step) % n_grp), "grp", step) for step in range(1, n_grp)
    ]
    attn, slabs, cots = gate(attend(qkv, text_len), slabs, cots)
    zero_rows = lax.all_gather(slabs, ("x", "core", "rep"))

    heads = lax.all_to_all(attn.reshape(8, 2 * tok, HEAD), ("x", "core"), split_axis=0, concat_axis=0, tiled=True)
    csum = sum(jnp.where(source(step) == 0, 0.0, cots[step].astype(F32)) for step in range(n_grp))
    own_cot = sum(jnp.where(source(step) == 0, cots[step], 0) for step in range(n_grp))
    csum = csum.astype(BF)
    csums = [csum] + [shift(csum, "grp", step) for step in range(1, n_grp)]
    level = lax.dynamic_slice_in_dim(gate_table, timestep[0, 0], 1, axis=0)

    def finish(first, own, other):
        at = slice(first * width, first * width + own.shape[1])
        proj = own + other.astype(F32)
        return (hidden[0, 0][:, at].astype(F32) + level[:, at] * proj).astype(BF)

    own_b, other_b = project(zl.reshape(1), heads, weight, 2, 2)
    heads, other_b = gate(heads, other_b)
    other_b = shift(other_b, "zl", 1)
    own_a, other_a = project(zl.reshape(1), heads, weight, 0, 2)
    other_a, csums[1], csums[3] = gate(other_a, csums[1], csums[3])
    other_a = shift(other_a, "zl", 1)
    own_b, csums = gate(own_b, csums)
    (out_b,) = gate(finish(2, own_b, other_b))
    parts = [send(out_b[:, :width], "grp", [(0, 2)]), send(out_b[:, width:], "grp", [(0, 3)])]
    out_a = finish(0, own_a, other_a)
    parts = [send(out_a[:, width:], "grp", [(0, 1)])] + parts
    out = jnp.concatenate([out_a, out_b], axis=1)
    csum_all = jnp.stack(ordered(csums, source))
    csum_x = lax.all_to_all(csum_all, "x", split_axis=0, concat_axis=0, tiled=True)
    control = out_a[:, :width]
    for j in range(1, n_grp):
        control = jnp.where(g == j, parts[j - 1], control)
    zero_rows = zero_rows.reshape(n_x, 2, n_rep, 2, slab, width)
    zero_flat = zero_rows.transpose(0, 3, 1, 2, 4, 5).reshape(n_grp, width, width)
    control, zero_rows, zero_flat, csum_x = gate(control, zero_rows, zero_flat, csum_x)

    resid = jnp.einsum("tr,brc->btc", control, zero_flat, preferred_element_type=F32).astype(BF)
    resid, control = gate(resid, control)
    resid = lax.all_to_all(resid, "grp", split_axis=0, concat_axis=0, tiled=True)
    mine_r = jnp.sum(resid.astype(F32), axis=0).astype(BF)
    ctl_x = ring_gather(control, "x")
    partial = grad_partial(x.reshape(1), ctl_x, csum_x)
    rows = width // 16
    partial = partial.reshape(2, 2, n_rep * rows, width).transpose(1, 0, 2, 3)
    mine = pick(partial, core).astype(F32)
    got = shift(pick(partial, 1 - core), "core", 1)
    halves = (mine + got.astype(F32)).astype(BF).reshape(2 * n_rep, rows, width)
    halves, csum_all = gate(halves, csum_all)
    ctrl_grad = with_zero(
        term_kernel, [csum_all, own_cot], zero_rows, (tok, width), "control_gradient"
    )
    halves, mine_r, ctrl_grad = gate(halves, mine_r, ctrl_grad)
    halves = lax.all_to_all(halves, ("zl", "rep"), split_axis=0, concat_axis=0, tiled=True)
    grad = jnp.sum(halves.astype(F32), axis=0).astype(BF)
    grad_zero = lax.ppermute(grad, ("grp", "x"), turn).astype(F32)
    blocks = [mine_r]
    for step in range(1, n_grp):
        pairs = [(i, (i + step) % n_grp) for i in range(n_grp) if (i + step) % n_grp]
        blocks.append(send(mine_r, "grp", pairs))
    blocks, grad_zero = gate(blocks, grad_zero)
    resid_all = jnp.concatenate(ordered(blocks, source), axis=1)
    final = jnp.where(is_control, out, (out.astype(F32) + resid_all.astype(F32)).astype(BF))

    return (final[None, None], ctrl_grad[None], grad_zero)


def solution(mesh):
    split = Mesh(mesh.devices.reshape(4, 4, 2, 2, 4), ("grp", "x", "zl", "core", "rep"))
    placed = (
        P("rep", "grp", SEQ, None),
        P("rep", "grp", SEQ, None, None),
        P("rep", "grp", SEQ, None),
        P("rep", "grp"),
        P("rep", "grp"),
        P(),
        P(None, SEQ, "rep"),
        P(SEQ, "grp"),
        P("rep", "grp", SEQ, None),
    )
    return jax.shard_map(
        shards,
        mesh=split,
        in_specs=placed,
        out_specs=(P("rep", "grp", SEQ, None), P("rep", SEQ, "grp"), P((*SEQ, "rep"), "grp")),
        check_vma=False,
    )
```

```python
import functools
import math

import jax
import jax.numpy as jnp
from jax import lax
from jax.experimental import pallas as pl
from jax.experimental.pallas import tpu as pltpu
from jax.sharding import Mesh, PartitionSpec as P

H = 16
HEAD = 128
SIZES = {"grp": 4, "x": 4, "zl": 2, "core": 2, "rep": 4}
SEQ = ("x", "zl", "core")
BF = jnp.bfloat16
F32 = jnp.float32
MIB = 1 << 20


def send(value, axis, pairs):
    return lax.ppermute(value, axis, pairs)


def shift(value, axis, step):
    n = SIZES[axis]
    return lax.ppermute(value, axis, [(i, (i + step) % n) for i in range(n)])


def attend_kernel(tlen_ref, q_ref, k_ref, v_ref, o_ref, wide_ref, *, text_slots, scale):
    @pl.when(pl.program_id(0) == 0)
    def _():
        length = wide_ref.shape[0]
        wide_ref[:, :HEAD] = v_ref[...].reshape(length, HEAD)
        wide_ref[:, HEAD:] = jnp.ones((length, HEAD), BF)

    length = wide_ref.shape[0]
    k = k_ref[...].reshape(length, HEAD)
    factor = scale * math.log2(math.e)
    blocks, rows, _ = q_ref.shape
    for at in range(0, blocks, 2):
        q = q_ref[at : at + 2].reshape(2 * rows, HEAD)
        s = lax.dot_general(q, k, (((1,), (1,)), ((), ())), preferred_element_type=F32)
        place = lax.broadcasted_iota(jnp.int32, (2 * rows, text_slots), 1)
        head = jnp.where(place < tlen_ref[0, 0], s[:, :text_slots], -jnp.inf)
        tail = s[:, text_slots:]
        top = jnp.maximum(
            jnp.max(head, axis=1, keepdims=True), jnp.max(tail, axis=1, keepdims=True)
        )
        p_head = jnp.exp2((head - top) * factor).astype(BF)
        p_tail = jnp.exp2((tail - top) * factor).astype(BF)
        both = jnp.dot(p_head, wide_ref[:text_slots, :], preferred_element_type=F32) + jnp.dot(
            p_tail, wide_ref[text_slots:, :], preferred_element_type=F32
        )
        result = (both[:, :HEAD] / both[:, HEAD:]).astype(BF)
        o_ref[at // 4, 0, at % 4 // 2] = result[:rows]
        o_ref[at // 4, 1, at % 4 // 2] = result[rows:]


def attend(qkv, tlen):
    blocks, _, per, _ = qkv.shape
    length = blocks * per
    q_blocks = 8
    rows = q_blocks * per
    whole = lambda part: pl.BlockSpec((blocks, None, per, HEAD), lambda i: (0, part, 0, 0))
    return pl.pallas_call(
        functools.partial(attend_kernel, text_slots=length // 8, scale=HEAD ** -0.5),
        grid=(length // rows,),
        in_specs=[
            pl.BlockSpec(memory_space=pltpu.SMEM),
            pl.BlockSpec((q_blocks, None, per, HEAD), lambda i: (i, 0, 0, 0)),
            whole(1),
            whole(2),
        ],
        out_specs=pl.BlockSpec((q_blocks // 4, 2, 2, per, HEAD), lambda i: (i, 0, 0, 0, 0)),
        out_shape=jax.ShapeDtypeStruct((blocks // 4, 2, 2, per, HEAD), BF),
        scratch_shapes=[pltpu.VMEM((length, 2 * HEAD), BF)],
        compiler_params=pltpu.CompilerParams(vmem_limit_bytes=56 * MIB),
        cost_estimate=pl.CostEstimate(
            flops=6 * length * length * HEAD,
            bytes_accessed=8 * length * HEAD,
            transcendentals=length * length,
        ),
        name="attend",
    )(tlen, qkv, qkv, qkv)


def project_kernel(zl_ref, a_ref, w_ref, own_ref, other_ref, a_held, wide_ref, held, sems, *, first):
    heads, half = held.shape[0], own_ref.shape[0]
    count, _, width = held.shape[1:]
    load = pltpu.make_async_copy(a_ref, a_held, sems.at[heads])
    load.start()
    copies = [
        pltpu.make_async_copy(w_ref.at[h, pl.ds(first, count)], held.at[h], sems.at[h])
        for h in range(heads)
    ]
    for copy in copies:
        copy.start()
    mine = pl.multiple_of(zl_ref[0] * half, half)
    theirs = pl.multiple_of((1 - zl_ref[0]) * half, half)
    load.wait()
    for h in range(heads):
        lanes = slice(h * HEAD, (h + 1) * HEAD)
        wide_ref[:half, lanes] = a_held[h, pl.ds(mine, half), :]
        wide_ref[half:, lanes] = a_held[h, pl.ds(theirs, half), :]
    for copy in copies:
        copy.wait()
    for j in range(count):
        w = held[:, j].reshape(heads * HEAD, width)
        total = jnp.dot(wide_ref[...], w, preferred_element_type=F32)
        lanes = slice(j * width, (j + 1) * width)
        own_ref[:, lanes] = total[:half]
        other_ref[:, lanes] = total[half:].astype(BF)


def project(zl, attn, weight, first, count):
    heads, rows, _ = attn.shape
    _, _, depth, width = weight.shape
    half = rows // 2
    vmem, anywhere = pl.BlockSpec(memory_space=pltpu.VMEM), pl.BlockSpec(memory_space=pl.ANY)
    return pl.pallas_call(
        functools.partial(project_kernel, first=first),
        in_specs=[pl.BlockSpec(memory_space=pltpu.SMEM), anywhere, anywhere],
        out_specs=[vmem, vmem],
        out_shape=[
            jax.ShapeDtypeStruct((half, count * width), F32),
            jax.ShapeDtypeStruct((half, count * width), BF),
        ],
        scratch_shapes=[
            pltpu.VMEM(attn.shape, BF),
            pltpu.VMEM((rows, heads * HEAD), BF),
            pltpu.VMEM((heads, count, depth, width), BF),
            pltpu.SemaphoreType.DMA((heads + 1,)),
        ],
        compiler_params=pltpu.CompilerParams(vmem_limit_bytes=16 * MIB),
        cost_estimate=pl.CostEstimate(
            flops=2 * rows * heads * HEAD * count * width,
            bytes_accessed=2 * heads * HEAD * count * width,
            transcendentals=0,
        ),
        name="project",
    )(zl, attn, weight)


def ring_gather(value, axis):
    return [value] + [shift(value, axis, step) for step in range(1, 4)]


def gate(*values):
    return lax.optimization_barrier(values)


def fetch_zero(zero_ref, held, sems):
    copies = []
    for x in range(4):
        for core in range(2):
            for rep in range(4):
                target = held.at[x, :, core, rep]
                copies.append(pltpu.make_async_copy(zero_ref.at[x, core, rep], target, sems.at[x, core, rep]))
    for copy in copies:
        copy.start()
    return copies


def block_of(held, copies, j):
    for copy in copies[8 * j : 8 * (j + 1)]:
        copy.wait()
    width = held.shape[-1]
    return held[j].reshape(width, width)


def term_kernel(csum_ref, cot_ref, zero_ref, o_ref, held, sems):
    copies = fetch_zero(zero_ref, held, sems)
    total = 0.0
    for j in range(4):
        term = lax.dot_general(
            csum_ref[j],
            block_of(held, copies, j),
            (((1,), (1,)), ((), ())),
            preferred_element_type=F32,
        )
        if j == 0:
            term = term + cot_ref[...].astype(F32)
        total = total + term.astype(BF).astype(F32)
    o_ref[...] = total.astype(BF)


def with_zero(kernel, dense, zero, shape, name):
    _, _, reps, _, slab, width = zero.shape
    vmem = pl.BlockSpec(memory_space=pltpu.VMEM)
    return pl.pallas_call(
        kernel,
        in_specs=[vmem] * len(dense) + [pl.BlockSpec(memory_space=pl.ANY)],
        out_specs=vmem,
        out_shape=jax.ShapeDtypeStruct(shape, BF),
        scratch_shapes=[
            pltpu.VMEM((4, 2, 2, reps, slab, width), BF),
            pltpu.SemaphoreType.DMA((4, 2, reps)),
        ],
        compiler_params=pltpu.CompilerParams(vmem_limit_bytes=16 * MIB),
        cost_estimate=pl.CostEstimate(
            flops=8 * shape[-2] * width * width, bytes_accessed=8 * width * width, transcendentals=0
        ),
        name=name,
    )(*dense, zero)


def grad_kernel(x_ref, *refs):
    pieces, csum_ref, (o_ref, ctl_ref, sum_ref, sems) = refs[:4], refs[4], refs[5:]
    rows = pieces[0].shape[0]
    copies = [pltpu.make_async_copy(csum_ref, sum_ref, sems.at[4])]
    for step, piece in enumerate(pieces):
        start = pl.multiple_of(lax.rem(x_ref[0] + 4 - step, 4) * rows, rows)
        copies.append(pltpu.make_async_copy(piece, ctl_ref.at[pl.ds(start, rows), :], sems.at[step]))
    for copy in copies:
        copy.start()
    for copy in copies:
        copy.wait()
    o_ref[...] = lax.dot_general(
        ctl_ref[...],
        sum_ref[...].reshape(ctl_ref.shape),
        (((0,), (0,)), ((), ())),
        preferred_element_type=F32,
    ).astype(BF)


def grad_partial(x, ctl, csum):
    blocks, rows, width = csum.shape
    return pl.pallas_call(
        grad_kernel,
        in_specs=[pl.BlockSpec(memory_space=pltpu.SMEM)]
        + [pl.BlockSpec(memory_space=pl.ANY)] * 5,
        out_specs=pl.BlockSpec(memory_space=pltpu.VMEM),
        out_shape=jax.ShapeDtypeStruct((width, width), BF),
        scratch_shapes=[
            pltpu.VMEM((blocks * rows, width), BF),
            pltpu.VMEM(csum.shape, BF),
            pltpu.SemaphoreType.DMA((5,)),
        ],
        compiler_params=pltpu.CompilerParams(vmem_limit_bytes=16 * MIB),
        cost_estimate=pl.CostEstimate(
            flops=8 * rows * width * width, bytes_accessed=18 * rows * width, transcendentals=0
        ),
        name="grad_partial",
    )(x, *ctl, csum)


def pick(blocks, index):
    return lax.dynamic_index_in_dim(blocks, index, 0, keepdims=False)


def ordered(blocks, source):
    result = []
    for j in range(len(blocks)):
        block = blocks[0]
        for step in range(1, len(blocks)):
            block = jnp.where(source(step) == j, blocks[step], block)
        result.append(block)
    return result


def shards(hidden, queries_keys, values, text_len, timestep, gate_table, w_out, w_zero, cotangent):
    g = lax.axis_index("grp")
    x = lax.axis_index("x")
    core = lax.axis_index("core")
    rep = lax.axis_index("rep")
    zl = lax.axis_index("zl")
    is_control = g == 0
    n_grp, n_x, n_rep = SIZES["grp"], SIZES["x"], SIZES["rep"]
    tok, width = hidden.shape[2], w_zero.shape[1]

    def source(step):
        return (g - step) % n_grp

    pair = queries_keys[0, 0].reshape(tok, 2, H, HEAD).transpose(2, 1, 0, 3)
    vals = values[0, 0].reshape(tok, 1, H, HEAD).transpose(2, 1, 0, 3)
    qkv, w_both = gate(jnp.concatenate([pair, vals], axis=1), w_out)
    w_sel = jnp.where(is_control, w_both[0], w_both[1])
    weight = lax.all_gather(w_sel, ("x", "core", "rep")).reshape(8, n_rep, *w_sel.shape)

    qkv = lax.all_to_all(qkv, SEQ, split_axis=0, concat_axis=0, tiled=True)
    turn = [(i * n_grp + j, j * n_grp + i) for i in range(n_x) for j in range(n_grp)]
    slab = w_zero.shape[0] // n_rep
    zero_slab = lax.dynamic_slice_in_dim(w_zero, rep * slab, slab, axis=0)
    zero_slab = lax.ppermute(zero_slab, ("grp", "x"), turn)

    slab_other = shift(zero_slab, "zl", 1)
    slabs = jnp.stack(
        [jnp.where(zl == 0, zero_slab, slab_other), jnp.where(zl == 0, slab_other, zero_slab)]
    )
    qkv, slabs, cot = gate(qkv, slabs, cotangent[0, 0])

    def cot_block(index):
        return lax.dynamic_slice_in_dim(cot, index * width, width, axis=1)

    cots = [cot_block(g)] + [
        shift(cot_block((g + step) % n_grp), "grp", step) for step in range(1, n_grp)
    ]
    attn, slabs, cots = gate(attend(qkv, text_len), slabs, cots)
    zero_rows = lax.all_gather(slabs, ("x", "core", "rep"))

    heads = lax.all_to_all(attn.reshape(8, 2 * tok, HEAD), ("x", "core"), split_axis=0, concat_axis=0, tiled=True)
    csum = sum(jnp.where(source(step) == 0, 0.0, cots[step].astype(F32)) for step in range(n_grp))
    own_cot = sum(jnp.where(source(step) == 0, cots[step], 0) for step in range(n_grp))
    csum = csum.astype(BF)
    csums = [csum] + [shift(csum, "grp", step) for step in range(1, n_grp)]
    level = lax.dynamic_slice_in_dim(gate_table, timestep[0, 0], 1, axis=0)

    def finish(first, own, other):
        at = slice(first * width, first * width + own.shape[1])
        proj = own + other.astype(F32)
        return (hidden[0, 0][:, at].astype(F32) + level[:, at] * proj).astype(BF)

    own_b, other_b = project(zl.reshape(1), heads, weight, 2, 2)
    heads, other_b = gate(heads, other_b)
    other_b = shift(other_b, "zl", 1)
    own_a, other_a = project(zl.reshape(1), heads, weight, 0, 2)
    other_a, csums[1], csums[3] = gate(other_a, csums[1], csums[3])
    other_a = shift(other_a, "zl", 1)
    own_b, csums = gate(own_b, csums)
    (out_b,) = gate(finish(2, own_b, other_b))
    parts = [send(out_b[:, :width], "grp", [(0, 2)]), send(out_b[:, width:], "grp", [(0, 3)])]
    out_a = finish(0, own_a, other_a)
    parts = [send(out_a[:, width:], "grp", [(0, 1)])] + parts
    out = jnp.concatenate([out_a, out_b], axis=1)
    csum_all = jnp.stack(ordered(csums, source))
    csum_x = lax.all_to_all(csum_all, "x", split_axis=0, concat_axis=0, tiled=True)
    control = out_a[:, :width]
    for j in range(1, n_grp):
        control = jnp.where(g == j, parts[j - 1], control)
    zero_rows = zero_rows.reshape(n_x, 2, n_rep, 2, slab, width)
    zero_flat = zero_rows.transpose(0, 3, 1, 2, 4, 5).reshape(n_grp, width, width)
    control, zero_rows, zero_flat, csum_x = gate(control, zero_rows, zero_flat, csum_x)

    resid = jnp.einsum("tr,brc->btc", control, zero_flat, preferred_element_type=F32).astype(BF)
    resid, control = gate(resid, control)
    resid = lax.all_to_all(resid, "grp", split_axis=0, concat_axis=0, tiled=True)
    mine_r = jnp.sum(resid.astype(F32), axis=0).astype(BF)
    ctl_x = ring_gather(control, "x")
    partial = grad_partial(x.reshape(1), ctl_x, csum_x)
    rows = width // 16
    partial = partial.reshape(2, 2, n_rep * rows, width).transpose(1, 0, 2, 3)
    mine = pick(partial, core).astype(F32)
    got = shift(pick(partial, 1 - core), "core", 1)
    halves = (mine + got.astype(F32)).astype(BF).reshape(2 * n_rep, rows, width)
    halves, csum_all = gate(halves, csum_all)
    ctrl_grad = with_zero(
        term_kernel, [csum_all, own_cot], zero_rows, (tok, width), "control_gradient"
    )
    halves, mine_r, ctrl_grad = gate(halves, mine_r, ctrl_grad)
    halves = lax.all_to_all(halves, ("zl", "rep"), split_axis=0, concat_axis=0, tiled=True)
    grad = jnp.sum(halves.astype(F32), axis=0).astype(BF)
    grad_zero = lax.ppermute(grad, ("grp", "x"), turn).astype(F32)
    blocks = [mine_r]
    for step in range(1, n_grp):
        pairs = [(i, (i + step) % n_grp) for i in range(n_grp) if (i + step) % n_grp]
        blocks.append(send(mine_r, "grp", pairs))
    blocks, grad_zero = gate(blocks, grad_zero)
    resid_all = jnp.concatenate(ordered(blocks, source), axis=1)
    final = jnp.where(is_control, out, (out.astype(F32) + resid_all.astype(F32)).astype(BF))

    return (final[None, None], ctrl_grad[None], grad_zero)


def solution(mesh):
    split = Mesh(mesh.devices.reshape(4, 4, 2, 2, 4), ("grp", "x", "zl", "core", "rep"))
    placed = (
        P("rep", "grp", SEQ, None),
        P("rep", "grp", SEQ, None, None),
        P("rep", "grp", SEQ, None),
        P("rep", "grp"),
        P("rep", "grp"),
        P(),
        P(None, SEQ, "rep"),
        P(SEQ, "grp"),
        P("rep", "grp", SEQ, None),
    )
    return jax.shard_map(
        shards,
        mesh=split,
        in_specs=placed,
        out_specs=(P("rep", "grp", SEQ, None), P("rep", SEQ, "grp"), P((*SEQ, "rep"), "grp")),
        check_vma=False,
    )
```
